256 devices in a mesh: pos: 16 (over y, z_lo, core), mom: 16 (over x, z_hi).
Axes of the slice: x: 4, y: 4, z: 8 (z_hi: 4, z_lo: 2; z = z_hi * 2 + z_lo), core: 2. Of those that a mesh axis runs over, the one named last changes fastest.
Arguments:
- quasi_probability_grid: float32 [2, 2048, 8192], P(None, 'pos', 'mom'), may hold values from 0 to 2
- potential_energy_map: float32 [2, 2048], P(None, 'pos'), may hold values from -3 to 3
- contact_inflow_states: float32 [2, 2, 8192], P(None, None, 'mom'), may hold values from 0 to 2
- crystal_kelvin_field: float32 [2048], P('pos'), may hold values from 0.6 to 1.6
- area_index_map: int32 [2048], P('pos'), may hold values from 0 to 3
- damping_ratio_per_step: float32 [4], replicated, may hold values from 0.05 to 0.5
- equilibrium_populace: float32 [4], replicated, may hold values from 0.5 to 2
- conductance_per_step: float32 [4], replicated, may hold values from 0.05 to 0.45
Outputs:
- wigner_updated: float32 [2, 2048, 8192], P(None, 'pos', 'mom')
- phonon_warmth_updated: float32 [2048], P('pos')
The draws below stay inside these ranges and needn't reach their ends.
All inputs are finite; a program needn't handle non-finite values.
Results may differ from the reference program's by a relative error of at most 0.0003.
Values sent between devices are 32-bit elements; how exact they have to be, the bound alone decides.
No kernel may reach another device: no remote copies, remote signals or barrier semaphores. Data moves between devices by JAX's collectives and lax.ppermute only.
A program may use at most 64 MiB of HBM per device.

```python
import math
import jax
import jax.numpy as jnp
from jax import lax

K = 8192
SUB = 2
AREA_KINDS = 4
SPOT_TOTAL = 128
CHANNEL_SPOTS = 2048
STRIDE = 1
N_POS = 16


def set_ends(array, own_key, smallest, largest):
    place = [jax.random.randint(jax.random.fold_in(own_key, axis), (), 0, length) for axis, length in enumerate(array.shape)]
    longest = array.shape.index(max(array.shape))
    beside = place[:longest] + [(place[longest] + 1) % array.shape[longest]] + place[longest + 1:]
    return array.at[tuple(place)].set(smallest).at[tuple(beside)].set(largest)


def block_levels(own_key, shape, shards, low, top_value):
    loudness = 1.0
    for position, blocks in shards:
        steps = jax.random.uniform(jax.random.fold_in(jax.random.fold_in(own_key, 6), position), (blocks,), jnp.float32, low / len(shards), top_value / len(shards))
        loudness = loudness * jnp.repeat(jnp.exp(steps), shape[position] // blocks).reshape((-1,) + (1,) * (len(shape) - 1 - position))
    return loudness


def gaussian(stream_key, extent, spread, most, split=(), kind=jnp.bfloat16):
    array = jax.random.normal(stream_key, extent, jnp.float32) * spread
    if len(split) > 0:
        array = block_levels(stream_key, extent, split, -0.22, 0.18) * array
    return jnp.clip(array, min=-most, max=most).astype(kind)


def setup_inputs(seed: int = 0) -> dict:
    seeds = jax.random.split(jax.random.key(seed), 9)
    quasi_probability_grid = jnp.clip(2.0 * jax.random.uniform(seeds[0], (SUB, CHANNEL_SPOTS, K), jnp.float32) ** block_levels(seeds[0], (SUB, CHANNEL_SPOTS, K), ((1, 16), (2, 16)), -0.2, 0.2), 0.0, 2.0)
    potential_energy_map = gaussian(seeds[1], (SUB, CHANNEL_SPOTS), 0.5, 3.0, ((1, 16),), jnp.float32)
    contact_inflow_states = jnp.clip(2.0 * jax.random.uniform(seeds[2], (SUB, 2, K), jnp.float32) ** block_levels(seeds[2], (SUB, 2, K), ((2, 16),), -0.2, 0.2), 0.0, 2.0)
    crystal_kelvin_field = jnp.clip(0.6 + 1.0 * jax.random.uniform(seeds[3], (CHANNEL_SPOTS,), jnp.float32) ** block_levels(seeds[3], (CHANNEL_SPOTS,), ((0, 16),), -0.2, 0.2), 0.6, 1.6)
    area_index_map = set_ends(jax.random.randint(seeds[4], (CHANNEL_SPOTS,), 0, AREA_KINDS), jax.random.fold_in(seeds[4], 1), 0, AREA_KINDS - 1).astype(jnp.int32)
    damping_ratio_per_step = jnp.clip(jnp.exp(jax.random.uniform(seeds[5], (AREA_KINDS,), jnp.float32, math.log(0.05), math.log(0.5))), 0.05, 0.5)
    equilibrium_populace = jnp.clip(jnp.exp(jax.random.uniform(seeds[6], (AREA_KINDS,), jnp.float32, math.log(0.5), math.log(2.0))), 0.5, 2.0)
    conductance_per_step = jnp.clip(jax.random.uniform(seeds[7], (AREA_KINDS,), jnp.float32, 0.05, 0.45), 0.05, 0.45)
    return {"quasi_probability_grid": quasi_probability_grid, "potential_energy_map": potential_energy_map, "contact_inflow_states": contact_inflow_states, "crystal_kelvin_field": crystal_kelvin_field, "area_index_map": area_index_map, "damping_ratio_per_step": damping_ratio_per_step, "equilibrium_populace": equilibrium_populace, "conductance_per_step": conductance_per_step}


courant = 0.9
energy_top = 3.0
energy_shift = 0.25
band_offset = 0.5
potential_gain = 0.5
heat_gain = 0.5
heat_outflow = 0.1


def reference(quasi_probability_grid, potential_energy_map, contact_inflow_states, crystal_kelvin_field, area_index_map, damping_ratio_per_step, equilibrium_populace, conductance_per_step):
    mom_grid = jnp.arange(K, dtype=jnp.float32)
    unit_mom = (2.0 * mom_grid + 1.0) / K - 1.0
    velocity = courant * unit_mom
    band_minimum = energy_top * (unit_mom + energy_shift) ** 2
    indicator_matrix = (area_index_map[None, :] == jnp.arange(AREA_KINDS, dtype=jnp.int32)[:, None]).astype(jnp.float32)
    relax_rows = jnp.sum(indicator_matrix * damping_ratio_per_step[:, None], axis=0)
    populace_matrix = jnp.sum(indicator_matrix * equilibrium_populace[:, None], axis=0)
    coupling_slices = jnp.sum(indicator_matrix * conductance_per_step[:, None], axis=0)
    mode_minimum = band_offset * jnp.arange(SUB, dtype=jnp.float32)
    dist_index = jnp.arange(K, dtype=jnp.int32)
    signed = jnp.where(dist_index < K // 2, dist_index, dist_index - K)

    def one_block(block_index):
        front_slice = block_index * SPOT_TOTAL
        center = lax.dynamic_slice_in_dim(quasi_probability_grid, front_slice, SPOT_TOTAL, 1)
        prev_row = lax.dynamic_slice_in_dim(quasi_probability_grid, jnp.maximum(front_slice - 1, 0), 1, 1)
        next_row = lax.dynamic_slice_in_dim(quasi_probability_grid, jnp.minimum(front_slice + SPOT_TOTAL, CHANNEL_SPOTS - 1), 1, 1)
        prev_row = jnp.where(block_index == 0, contact_inflow_states[:, 0:1, :], prev_row)
        next_row = jnp.where(block_index == N_POS - 1, contact_inflow_states[:, 1:2, :], next_row)
        below_rows = jnp.concatenate([prev_row, center[:, :-1, :]], axis=1)
        above_rows = jnp.concatenate([center[:, 1:, :], next_row], axis=1)
        drift_term = jnp.where(velocity > 0, -velocity * (center - below_rows), -velocity * (above_rows - center))
        warmth_piece = lax.dynamic_slice_in_dim(crystal_kelvin_field, front_slice, SPOT_TOTAL, 0)
        dens_block = lax.dynamic_slice_in_dim(populace_matrix, front_slice, SPOT_TOTAL, 0)
        relax_block = lax.dynamic_slice_in_dim(relax_rows, front_slice, SPOT_TOTAL, 0)
        equilibrium = dens_block[None, :, None] * jnp.exp(
            -(band_minimum[None, None, :] + mode_minimum[:, None, None]) / warmth_piece[None, :, None])
        places = front_slice + jnp.arange(SPOT_TOTAL, dtype=jnp.int32)
        ahead_index = jnp.clip(places[:, None] + STRIDE * signed[None, :], 0, CHANNEL_SPOTS - 1).astype(jnp.int32)
        behind_index = jnp.clip(places[:, None] - STRIDE * signed[None, :], 0, CHANNEL_SPOTS - 1).astype(jnp.int32)
        pot_diff = jnp.take(potential_energy_map, ahead_index, axis=1) - jnp.take(potential_energy_map, behind_index, axis=1)
        spectrum = jnp.fft.ifft(center, axis=-1) * K
        nonlocal_part = (potential_gain / K) * jnp.imag(jnp.fft.fft(pot_diff * spectrum, axis=-1))
        updated = center + drift_term + nonlocal_part - relax_block[None, :, None] * (center - equilibrium)
        joule_input = (heat_gain / K) * relax_block * jnp.sum(band_minimum[None, None, :] * (center - equilibrium), axis=(0, 2))
        return updated, joule_input

    new_blocks, heat_blocks = lax.map(one_block, jnp.arange(N_POS, dtype=jnp.int32))
    wigner_updated = jnp.transpose(new_blocks, (1, 0, 2, 3)).reshape(SUB, CHANNEL_SPOTS, K)
    joule_input = heat_blocks.reshape(CHANNEL_SPOTS)
    ones_margin = jnp.ones((1,), jnp.float32)
    warmth_padded_vector = jnp.concatenate([ones_margin, crystal_kelvin_field, ones_margin])
    phonon_warmth_updated = (crystal_kelvin_field + coupling_slices * (warmth_padded_vector[2:] - 2.0 * crystal_kelvin_field + warmth_padded_vector[:-2])
                        + joule_input - heat_outflow * (crystal_kelvin_field - 1.0))
    return wigner_updated, phonon_warmth_updated
```

```python
import functools

import jax
import jax.numpy as jnp
import numpy as np
from jax import lax
from jax.experimental import pallas as pl
from jax.experimental.pallas import tpu as pltpu
from jax.sharding import PartitionSpec as P

K = 8192
LANES = 128
RESIDUES = 64
ROWS = 16
FLAT = 72

courant = 0.9
energy_top = 3.0
energy_shift = 0.25
band_offset = 0.5
potential_gain = 0.5
heat_gain = 0.5
heat_outflow = 0.1

RESIDUE_LIST = [u1 + 8 * u0 for u1 in (1, 2, 3) for u0 in range(8)] + [4, 12, 20, 28, 0, 8, 16, 24, 32]
COUNT = len(RESIDUE_LIST)
PLACE = {u: n for n, u in enumerate(RESIDUE_LIST)}
ROOT = float(np.sqrt(0.5))


def tables():
    idx = np.arange(LANES)
    angle = 2.0 * np.pi / LANES * (idx[:, None] * idx[None, :] % LANES)
    cos, sin = np.cos(angle), np.sin(angle)
    ahead = np.block([[cos, sin], [-sin, cos]]).astype(np.float32)

    def parts(matrix):
        high = matrix.astype(jnp.bfloat16)
        low = (matrix - high.astype(np.float32)).astype(jnp.bfloat16)
        return np.stack([high, low])

    turn = 2.0 * np.pi / K * (np.array(RESIDUE_LIST)[:, None] * idx[None, :])
    twist = np.stack([np.cos(turn), np.sin(turn)], axis=1).astype(np.float32)
    return parts(ahead), parts(np.ascontiguousarray(ahead.T)), twist


def add(a, b):
    return (a[0] + b[0], a[1] + b[1])


def sub(a, b):
    return (a[0] - b[0], a[1] - b[1])


def times_i(a):
    return (-a[1], a[0])


def turned(a, angle):
    c, s = float(np.cos(angle)), float(np.sin(angle))
    return (a[0] * c - a[1] * s, a[0] * s + a[1] * c)


def real_8(f):
    a0, a1, b0, b1 = f[0] + f[4], f[0] - f[4], f[2] + f[6], f[2] - f[6]
    c0, c1, d0, d1 = f[1] + f[5], f[1] - f[5], f[3] + f[7], f[3] - f[7]
    even, odd = a0 + b0, c0 + d0
    less, more = ROOT * (c1 - d1), ROOT * (c1 + d1)
    return even + odd, (a1 + less, b1 + more), (a0 - b0, c0 - d0), (a1 - less, more - b1), even - odd


def back_8(x0, d1, d2, d3, x4):
    even, odd = x0 + x4, x0 - x4
    (r1, i1), (r2, i2), (r3, i3) = d1, d2, d3
    ea, eb = even + r2, even - r2
    sr, si = r1 + r3, i3 - i1
    oa, ob = odd - i2, odd + i2
    p, q = ROOT * (r1 - i1), ROOT * (r1 + i1)
    v, w = ROOT * (r3 + i3), ROOT * (r3 - i3)
    pv, wq = p - v, w - q
    return [ea + sr, oa + pv, eb + si, ob + wq, ea - sr, oa - pv, eb - si, ob - wq]


def complex_4(x):
    a, b, c, d = add(x[0], x[2]), sub(x[0], x[2]), add(x[1], x[3]), times_i(sub(x[1], x[3]))
    return [add(a, c), add(b, d), sub(a, c), sub(b, d)]


def complex_8(x):
    e, o = complex_4(x[0::2]), complex_4(x[1::2])
    o[1] = (ROOT * (o[1][0] - o[1][1]), ROOT * (o[1][0] + o[1][1]))
    o[2] = times_i(o[2])
    o[3] = (-ROOT * (o[3][0] + o[3][1]), ROOT * (o[3][0] - o[3][1]))
    return [add(e[n], o[n]) for n in range(4)] + [sub(e[n], o[n]) for n in range(4)]


def cs(n):
    return float(np.cos(np.pi * n / 8)), float(np.sin(np.pi * n / 8))


def odd_ahead(a):
    less = [None] + [a[q] - a[8 - q] for q in (1, 2, 3)]
    more = [None] + [a[q] + a[8 - q] for q in (1, 2, 3)]
    out = [None] * 4
    for u in (0, 1):
        n = 1 + 2 * u
        even_r = a[0] + less[2] * cs(2 * n)[0]
        odd_r = less[1] * cs(n)[0] + less[3] * cs(3 * n)[0]
        even_i = more[2] * cs(2 * n)[1]
        odd_i = more[1] * cs(n)[1] + more[3] * cs(3 * n)[1]
        even_i = even_i + a[4] if u == 0 else even_i - a[4]
        out[u] = (even_r + odd_r, odd_i + even_i)
        out[3 - u] = (even_r - odd_r, odd_i - even_i)
    return out


def odd_back(c):
    (r0, i0), (r1, i1), (r2, i2), (r3, i3) = c
    rp0, rm0, rp1, rm1 = r0 + r3, r0 - r3, r1 + r2, r1 - r2
    ip0, im0, ip1, im1 = i0 + i3, i0 - i3, i1 + i2, i1 - i2
    out = [None] * 8
    out[0] = rp0 + rp1
    out[4] = (i1 + i3) - (i0 + i2)
    for q in (1, 2, 3):
        (c0, s0), (c1, s1) = cs(q), cs(3 * q)
        if q % 2:
            cosines, sines = rm0 * c0 + rm1 * c1, ip0 * s0 + ip1 * s1
        else:
            cosines, sines = rp0 * c0 + rp1 * c1, im0 * s0 + im1 * s1
        out[q], out[8 - q] = cosines - sines, -cosines - sines
    return out


def split(value):
    high = value.astype(jnp.bfloat16)
    return high, (value - high.astype(jnp.float32)).astype(jnp.bfloat16)


def product(high, low, weights):
    dot = functools.partial(jnp.dot, preferred_element_type=jnp.float32)
    return dot(high, weights[0]) + (dot(high, weights[1]) + dot(low, weights[0]))


def transform_kernel(rows_ref, weight_ref, lattice_ref, gain_ref, ahead_ref, back_ref, twist_ref, out_ref,
                     stage, high, low, result):
    splits = rows_ref.shape[0]
    per = RESIDUES // splits

    lane = lax.broadcasted_iota(jnp.int32, (1, LANES), 1).astype(jnp.float32)

    def cell(q):
        n = (q % per) * LANES
        return rows_ref[q // per, :, n : n + LANES]

    total = jnp.zeros((ROWS, LANES), jnp.float32)
    for q0 in range(8):
        f = []
        for q1 in range(8):
            q = q1 * 8 + q0
            value = cell(q)
            unit = (2.0 * (lane + float(q * LANES)) + 1.0) / K - 1.0
            total = total + value * (energy_top * (unit + energy_shift) ** 2)
            f.append(value)
        x0, x1, x2, x3, x4 = real_8(f)
        for n, value in enumerate((x0, x1[0], x1[1], x2[0], x2[1], x3[0], x3[1], x4)):
            stage[q0 * 8 + n] = value
    heat = jnp.sum(total[:8] + total[8:], axis=1, keepdims=True)
    lattice = lattice_ref[...] + gain_ref[...] * heat

    def send(u, value):
        n = PLACE[u]
        real, imag = value
        c, s = twist_ref[n, 0:1, :], twist_ref[n, 1:2, :]
        if imag is None:
            real, imag = real * c, real * s
        else:
            real, imag = real * c - imag * s, real * s + imag * c
        for half, part in ((0, real), (1, imag)):
            h, l = split(part)
            place = (slice(n * ROWS, n * ROWS + ROWS), slice(half * LANES, half * LANES + LANES))
            high[place] = h
            low[place] = l

    for u1 in (1, 2, 3):
        x = [(stage[q0 * 8 + 2 * u1 - 1], stage[q0 * 8 + 2 * u1]) for q0 in range(8)]
        x = [x[0]] + [turned(x[q0], 2.0 * np.pi * q0 * u1 / 64) for q0 in range(1, 8)]
        for u0, value in enumerate(complex_8(x)):
            send(u1 + 8 * u0, value)
    for u0, value in enumerate(odd_ahead([stage[q0 * 8 + 7] for q0 in range(8)])):
        send(4 + 8 * u0, value)
    x0, x1, x2, x3, x4 = real_8([stage[q0 * 8] for q0 in range(8)])
    for u, value in ((0, (x0, None)), (8, x1), (16, x2), (24, x3), (32, (x4, None))):
        send(u, value)

    for n in range(0, COUNT, 11):
        rows = slice(n * ROWS, (n + 11) * ROWS)
        spectrum = product(high[rows], low[rows], ahead_ref)
        weight = weight_ref[rows]
        h0, l0 = split(spectrum[:, :LANES] * weight)
        h1, l1 = split(spectrum[:, LANES:] * weight)
        result[rows] = product(
            jnp.concatenate([h0, h1], axis=1), jnp.concatenate([l0, l1], axis=1), back_ref
        )

    def fetch(u):
        n = PLACE[u]
        rows = slice(n * ROWS, n * ROWS + ROWS)
        real, imag = result[rows, :LANES], result[rows, LANES:]
        c, s = twist_ref[n, 0:1, :], twist_ref[n, 1:2, :]
        return imag * c - real * s, real * c + imag * s

    for u1 in (1, 2, 3):
        d = complex_8([fetch(u1 + 8 * u0) for u0 in range(8)])
        for q0 in range(8):
            value = turned(d[q0], 2.0 * np.pi * q0 * u1 / 64) if q0 else d[0]
            stage[q0 * 8 + 2 * u1 - 1] = value[0]
            stage[q0 * 8 + 2 * u1] = value[1]
    for q0, value in enumerate(odd_back([fetch(4 + 8 * u0) for u0 in range(4)])):
        stage[q0 * 8 + 7] = value
    ends = back_8(fetch(0)[0], fetch(8), fetch(16), fetch(24), fetch(32)[0])
    for q0, value in enumerate(ends):
        stage[q0 * 8] = value
    for q0 in range(8):
        d = [stage[q0 * 8 + n] for n in range(8)]
        for q1, value in enumerate(back_8(d[0], (d[1], d[2]), (d[3], d[4]), (d[5], d[6]), d[7])):
            q = q1 * 8 + q0
            m, jb = q // per, q % per
            for b in range(2):
                n = (b * per + jb) * 8
                out_ref[m, n : n + 8, :] = value[b * 8 : b * 8 + 8]
    lattice = jnp.broadcast_to(lattice, (8, LANES))
    for m in range(splits):
        out_ref[m, 64:72, :] = lattice


def pack_kernel(first_ref, last_ref, profile_ref, kelvin_ref, out_ref):
    me = lax.axis_index("pos")
    for target in range(out_ref.shape[0]):
        for b in range(2):
            row = jnp.where(target > me, last_ref[b, 7:8, :], first_ref[b, 0:1, :])
            for n in range(4):
                out_ref[target, b * 4 + n : b * 4 + n + 1, :] = row[:, n * LANES : n * LANES + LANES]
        out_ref[target, 8:10, :] = profile_ref[...]
        out_ref[target, 10:11, :] = kelvin_ref[...]
        out_ref[target, 11:16, :] = jnp.zeros((5, LANES), jnp.float32)


def chosen(area, table_ref):
    value = jnp.zeros(area.shape, jnp.float32)
    for n in range(table_ref.shape[0]):
        value = value + jnp.where(area == n, table_ref[n], 0.0)
    return value


def potential_kernel(around_ref, kelvin_ref, area_ref, damping_ref, populace_ref, conductance_ref,
                     weight_ref, lattice_ref, gain_ref, ahead_t, behind_t, ahead_w, behind_w, column):
    spot, mom = lax.axis_index("pos"), lax.axis_index("mom")
    spots = around_ref.shape[0]
    start = spot * LANES + mom * 8
    lead = start // RESIDUES
    inner = pl.multiple_of(start % RESIDUES, 8)
    source = lax.broadcasted_iota(jnp.int32, (spots, LANES), 0)
    lane = lax.broadcasted_iota(jnp.int32, (spots, LANES), 1)
    mirror = (LANES - lane) % LANES
    window = ahead_w.shape[0]
    row_w = lax.broadcasted_iota(jnp.int32, (window, LANES), 0)
    lane_w = lax.broadcasted_iota(jnp.int32, (window, LANES), 1)
    carry = (inner + row_w) // RESIDUES - 1
    ahead_q = lead + carry + lane_w - jnp.where(lane_w >= RESIDUES, LANES, 0)
    behind_q = lead + carry - lane_w + jnp.where(lane_w >= RESIDUES, LANES, 0)
    cells = spots * LANES // RESIDUES

    for b in range(2):
        profile = around_ref[:, 8 + b, :]
        first, last = profile[0:1, 0:1], profile[spots - 1 : spots, LANES - 1 : LANES]

        def pick(place):
            pieces = []
            for h in range(2):
                chooser = jnp.where(place == 2 * source + h, 1.0, 0.0)
                full = lax.dot_general(
                    profile, chooser, (((0,), (0,)), ((), ())),
                    precision=lax.Precision.HIGHEST, preferred_element_type=jnp.float32,
                )
                pieces.append(full[h * RESIDUES : h * RESIDUES + RESIDUES])
            return pieces[0] + pieces[1]

        forward, backward = pick(lane), pick(mirror)
        for n, k in enumerate((-1, 0, 1)):
            rows = slice(n * RESIDUES, n * RESIDUES + RESIDUES)
            ahead_t[rows] = pltpu.roll(forward, (-k) % LANES, 1) if k else forward
            behind_t[rows] = pltpu.roll(backward, k % LANES, 1) if k else backward
        for table, wide, shift, q in (
            (ahead_t, ahead_w, (LANES - lead) % LANES, ahead_q),
            (behind_t, behind_w, lead, behind_q),
        ):
            value = pltpu.roll(table[pl.ds(inner, window), :], shift, 1)
            value = jnp.where(q < 0, first, value)
            wide[...] = jnp.where(q >= cells, last, value)
        for n, u in enumerate(RESIDUE_LIST):
            scale = potential_gain / K * (1.0 if u in (0, 32) else 2.0)
            ahead = ahead_w[RESIDUES + u : RESIDUES + u + 8, :]
            behind = behind_w[RESIDUES - u : RESIDUES - u + 8, :]
            weight_ref[n * ROWS + b * 8 : n * ROWS + b * 8 + 8, :] = scale * (ahead - behind)

    before = around_ref[jnp.maximum(spot - 1, 0), 10:11, LANES - 1 : LANES]
    after = around_ref[jnp.minimum(spot + 1, spots - 1), 10:11, 0:1]
    column[0:8, :] = jnp.where(spot == 0, 1.0, before) * jnp.ones((8, 1), jnp.float32)
    column[8:136, :] = kelvin_ref[...]
    column[136:144, :] = jnp.where(spot == spots - 1, 1.0, after) * jnp.ones((8, 1), jnp.float32)
    base = pl.multiple_of(mom * 8, 8)
    near = column[pl.ds(base, 24), :]
    lower, kelvin, upper = near[7:15], near[8:16], near[9:17]
    area = area_ref[pl.ds(base, 8), :]
    relax, dens, cond = chosen(area, damping_ref), chosen(area, populace_ref), chosen(area, conductance_ref)
    lane8 = lax.broadcasted_iota(jnp.int32, (1, LANES), 1).astype(jnp.float32)
    inverse = -1.0 / kelvin
    total = jnp.zeros((8, LANES), jnp.float32)
    for q in range(RESIDUES):
        unit = (2.0 * (lane8 + float(q * LANES)) + 1.0) / K - 1.0
        energy = energy_top * (unit + energy_shift) ** 2
        for b in range(2):
            total = total + energy * jnp.exp((energy + band_offset * b) * inverse)
    gain = heat_gain / K * relax
    lattice_ref[...] = (
        kelvin
        + cond * (upper - 2.0 * kelvin + lower)
        - heat_outflow * (kelvin - 1.0)
        - gain * dens * jnp.sum(total, axis=1, keepdims=True)
    )
    gain_ref[...] = gain


def local_kernel(grid_ref, around_ref, contact_ref, kelvin_ref, area_ref, damping_ref, populace_ref, out_ref):
    spot, mom = lax.axis_index("pos"), lax.axis_index("mom")
    spots = around_ref.shape[0]
    _, rows, count = grid_ref.shape
    place = lax.broadcasted_iota(jnp.int32, (1, LANES), 1)
    row = lax.broadcasted_iota(jnp.int32, (rows, LANES), 0)
    inverse = -1.0 / kelvin_ref[...]
    relax = chosen(area_ref[...], damping_ref)
    dens = relax * chosen(area_ref[...], populace_ref)
    left, right = jnp.maximum(spot - 1, 0), jnp.minimum(spot + 1, spots - 1)
    for n in range(count // LANES):
        lanes = slice(n * LANES, n * LANES + LANES)
        unit = (2.0 * (place + (mom * count + n * LANES)).astype(jnp.float32) + 1.0) / K - 1.0
        velocity = courant * unit
        energy = energy_top * (unit + energy_shift) ** 2
        for b in range(2):
            f = grid_ref[b, :, lanes]
            before = jnp.where(spot == 0, contact_ref[b, 0:1, lanes], around_ref[left, b * 4 + n : b * 4 + n + 1, :])
            after = jnp.where(
                spot == spots - 1, contact_ref[b, 1:2, lanes], around_ref[right, b * 4 + n : b * 4 + n + 1, :]
            )
            below = jnp.where(row == 0, before, pltpu.roll(f, 1, 0))
            above = jnp.where(row == rows - 1, after, pltpu.roll(f, rows - 1, 0))
            drift = velocity * jnp.where(velocity > 0, below - f, f - above)
            settled = dens * jnp.exp((energy + band_offset * b) * inverse)
            out_ref[b, :, lanes] = f + drift - relax * f + settled


def final_kernel(base_ref, back_ref, out_ref, lattice_ref):
    splits = back_ref.shape[0]
    lane = lax.broadcasted_iota(jnp.int32, (8, LANES), 1)
    row = lax.broadcasted_iota(jnp.int32, (8, LANES), 0)
    total = jnp.zeros((8, LANES), jnp.float32)
    for m in range(splits):
        rows = slice(m * 8, m * 8 + 8)
        for b in range(2):
            for n in range(4):
                lanes = slice(n * LANES, n * LANES + LANES)
                start = (b * 4 + n) * 8
                out_ref[b, rows, lanes] = base_ref[b, rows, lanes] + back_ref[m, start : start + 8, :]
        total = total + jnp.where(lane == m * 8 + row, back_ref[m, 64:72, :], 0.0)
    lattice_ref[...] = jnp.sum(total, axis=0, keepdims=True)


VM = pl.BlockSpec(memory_space=pltpu.VMEM)
SM = pl.BlockSpec(memory_space=pltpu.SMEM)


def call(kernel, outs, specs, flops=0, moved=0, scratch=(), **more):
    return pl.pallas_call(
        kernel,
        out_shape=outs,
        in_specs=specs,
        out_specs=jax.tree.map(lambda _: VM, outs),
        scratch_shapes=list(scratch),
        compiler_params=pltpu.CompilerParams(vmem_limit_bytes=32 * 2**20),
        cost_estimate=pl.CostEstimate(flops=flops, bytes_accessed=moved, transcendentals=0),
        **more,
    )


def f32(*shape):
    return jax.ShapeDtypeStruct(shape, jnp.float32)


def body(grid, potential, contact, kelvin, area, damping, populace, conductance):
    bands, rows, count = grid.shape
    spots, splits = lax.axis_size("pos"), lax.axis_size("mom")
    share = rows // splits
    ahead, back, twist = tables()

    parts = grid.reshape(bands, splits, share, count).transpose(1, 0, 2, 3).reshape(splits, bands * share, count)
    full = lax.all_to_all(parts, "mom", split_axis=0, concat_axis=0)

    packed = pl.pallas_call(
        pack_kernel,
        grid=(1,),
        out_shape=f32(spots, 16, LANES),
        in_specs=[
            pl.BlockSpec((bands, 8, count), lambda i: (0, 0, 0)),
            pl.BlockSpec((bands, 8, count), lambda i: (0, rows // 8 - 1, 0)),
            pl.BlockSpec((bands, rows), lambda i: (0, 0)),
            pl.BlockSpec((1, rows), lambda i: (0, 0)),
        ],
        out_specs=pl.BlockSpec((spots, 16, LANES), lambda i: (0, 0, 0)),
    )(grid, grid, potential, kelvin.reshape(1, rows))
    around = lax.all_to_all(packed, "pos", split_axis=0, concat_axis=0)

    kelvin_col, area_col = kelvin.reshape(rows, 1), area.reshape(rows, 1)
    weight, lattice, gain = call(
        potential_kernel,
        (f32(COUNT * ROWS, LANES), f32(8, 1), f32(8, 1)),
        [VM, VM, VM, SM, SM, SM],
        flops=10**7,
        moved=2**20,
        scratch=[
            pltpu.VMEM((3 * RESIDUES, LANES), jnp.float32),
            pltpu.VMEM((3 * RESIDUES, LANES), jnp.float32),
            pltpu.VMEM((136, LANES), jnp.float32),
            pltpu.VMEM((136, LANES), jnp.float32),
            pltpu.VMEM((144, 1), jnp.float32),
        ],
    )(around, kelvin_col, area_col, damping, populace, conductance)
    base = call(
        local_kernel, f32(bands, rows, count), [VM, VM, VM, VM, VM, SM, SM], flops=10**7, moved=2**21
    )(grid, around, contact, kelvin_col, area_col, damping, populace)

    messages = call(
        transform_kernel,
        f32(splits, FLAT, LANES),
        [VM] * 7,
        flops=10**9,
        moved=2**21,
        scratch=[
            pltpu.VMEM((RESIDUES, ROWS, LANES), jnp.float32),
            pltpu.VMEM((COUNT * ROWS, 2 * LANES), jnp.bfloat16),
            pltpu.VMEM((COUNT * ROWS, 2 * LANES), jnp.bfloat16),
            pltpu.VMEM((COUNT * ROWS, 2 * LANES), jnp.float32),
        ],
    )(full, weight, lattice, gain, jnp.asarray(ahead), jnp.asarray(back), jnp.asarray(twist))
    received = lax.all_to_all(messages, "mom", split_axis=0, concat_axis=0)
    updated, warmth = call(
        final_kernel, (f32(bands, rows, count), f32(1, rows)), [VM, VM], flops=10**6, moved=2**21
    )(base, received)
    return updated, warmth.reshape(rows)


def solution(mesh):
    return jax.shard_map(
        body,
        mesh=mesh,
        in_specs=(
            P(None, "pos", "mom"),
            P(None, "pos"),
            P(None, None, "mom"),
            P("pos"),
            P("pos"),
            P(),
            P(),
            P(),
        ),
        out_specs=(P(None, "pos", "mom"), P("pos")),
        check_vma=False,
    )
```

```python
import functools

import jax
import jax.numpy as jnp
import numpy as np
from jax import lax
from jax.experimental import pallas as pl
from jax.experimental.pallas import tpu as pltpu
from jax.sharding import PartitionSpec as P

K = 8192
LANES = 128
RESIDUES = 64
ROWS = 16
QUAD = (0, -1, 1, 2)
FLAT = 72

courant = 0.9
energy_top = 3.0
energy_shift = 0.25
band_offset = 0.5
potential_gain = 0.5
heat_gain = 0.5
heat_outflow = 0.1

RESIDUE_LIST = [u1 + 8 * u0 for u1 in (1, 2, 3) for u0 in range(8)] + [4, 12, 20, 28, 0, 8, 16, 24, 32]
COUNT = len(RESIDUE_LIST)
PLACE = {u: n for n, u in enumerate(RESIDUE_LIST)}
ROOT = float(np.sqrt(0.5))


def tables():
    idx = np.arange(LANES)
    angle = 2.0 * np.pi / LANES * (idx[:, None] * idx[None, :] % LANES)
    cos, sin = np.cos(angle), np.sin(angle)
    ahead = np.block([[cos, sin], [-sin, cos]]).astype(np.float32)

    def parts(matrix):
        high = matrix.astype(jnp.bfloat16)
        low = (matrix - high.astype(np.float32)).astype(jnp.bfloat16)
        return np.stack([high, low])

    turn = 2.0 * np.pi / K * (np.array(RESIDUE_LIST)[:, None] * idx[None, :])
    twist = np.stack([np.cos(turn), np.sin(turn)], axis=1).astype(np.float32)
    return parts(ahead), parts(np.ascontiguousarray(ahead.T)), twist


def add(a, b):
    return (a[0] + b[0], a[1] + b[1])


def sub(a, b):
    return (a[0] - b[0], a[1] - b[1])


def times_i(a):
    return (-a[1], a[0])


def turned(a, angle):
    c, s = float(np.cos(angle)), float(np.sin(angle))
    return (a[0] * c - a[1] * s, a[0] * s + a[1] * c)


def real_8(f):
    a0, a1, b0, b1 = f[0] + f[4], f[0] - f[4], f[2] + f[6], f[2] - f[6]
    c0, c1, d0, d1 = f[1] + f[5], f[1] - f[5], f[3] + f[7], f[3] - f[7]
    even, odd = a0 + b0, c0 + d0
    less, more = ROOT * (c1 - d1), ROOT * (c1 + d1)
    return even + odd, (a1 + less, b1 + more), (a0 - b0, c0 - d0), (a1 - less, more - b1), even - odd


def back_8(x0, d1, d2, d3, x4):
    even, odd = x0 + x4, x0 - x4
    (r1, i1), (r2, i2), (r3, i3) = d1, d2, d3
    ea, eb = even + r2, even - r2
    sr, si = r1 + r3, i3 - i1
    oa, ob = odd - i2, odd + i2
    p, q = ROOT * (r1 - i1), ROOT * (r1 + i1)
    v, w = ROOT * (r3 + i3), ROOT * (r3 - i3)
    pv, wq = p - v, w - q
    return [ea + sr, oa + pv, eb + si, ob + wq, ea - sr, oa - pv, eb - si, ob - wq]


def complex_4(x):
    a, b, c, d = add(x[0], x[2]), sub(x[0], x[2]), add(x[1], x[3]), times_i(sub(x[1], x[3]))
    return [add(a, c), add(b, d), sub(a, c), sub(b, d)]


def complex_8(x):
    e, o = complex_4(x[0::2]), complex_4(x[1::2])
    o[1] = (ROOT * (o[1][0] - o[1][1]), ROOT * (o[1][0] + o[1][1]))
    o[2] = times_i(o[2])
    o[3] = (-ROOT * (o[3][0] + o[3][1]), ROOT * (o[3][0] - o[3][1]))
    return [add(e[n], o[n]) for n in range(4)] + [sub(e[n], o[n]) for n in range(4)]


def cs(n):
    return float(np.cos(np.pi * n / 8)), float(np.sin(np.pi * n / 8))


def odd_ahead(a):
    less = [None] + [a[q] - a[8 - q] for q in (1, 2, 3)]
    more = [None] + [a[q] + a[8 - q] for q in (1, 2, 3)]
    out = [None] * 4
    for u in (0, 1):
        n = 1 + 2 * u
        even_r = a[0] + less[2] * cs(2 * n)[0]
        odd_r = less[1] * cs(n)[0] + less[3] * cs(3 * n)[0]
        even_i = more[2] * cs(2 * n)[1]
        odd_i = more[1] * cs(n)[1] + more[3] * cs(3 * n)[1]
        even_i = even_i + a[4] if u == 0 else even_i - a[4]
        out[u] = (even_r + odd_r, odd_i + even_i)
        out[3 - u] = (even_r - odd_r, odd_i - even_i)
    return out


def odd_back(c):
    (r0, i0), (r1, i1), (r2, i2), (r3, i3) = c
    rp0, rm0, rp1, rm1 = r0 + r3, r0 - r3, r1 + r2, r1 - r2
    ip0, im0, ip1, im1 = i0 + i3, i0 - i3, i1 + i2, i1 - i2
    out = [None] * 8
    out[0] = rp0 + rp1
    out[4] = (i1 + i3) - (i0 + i2)
    for q in (1, 2, 3):
        (c0, s0), (c1, s1) = cs(q), cs(3 * q)
        if q % 2:
            cosines, sines = rm0 * c0 + rm1 * c1, ip0 * s0 + ip1 * s1
        else:
            cosines, sines = rp0 * c0 + rp1 * c1, im0 * s0 + im1 * s1
        out[q], out[8 - q] = cosines - sines, -cosines - sines
    return out


def split(value):
    high = value.astype(jnp.bfloat16)
    return high, (value - high.astype(jnp.float32)).astype(jnp.bfloat16)


def product(high, low, weights):
    dot = functools.partial(jnp.dot, preferred_element_type=jnp.float32)
    return dot(high, weights[0]) + (dot(high, weights[1]) + dot(low, weights[0]))


def transform_kernel(rows_ref, weight_ref, lattice_ref, gain_ref, ahead_ref, back_ref, twist_ref, out_ref,
                     stage, high, low, result):
    splits = rows_ref.shape[0]
    per = RESIDUES // splits

    lane = lax.broadcasted_iota(jnp.int32, (1, LANES), 1).astype(jnp.float32)

    def cell(q):
        n = (q % per) * LANES
        return rows_ref[q // per, :, n : n + LANES]

    total = jnp.zeros((ROWS, LANES), jnp.float32)
    for q0 in range(8):
        f = []
        for q1 in range(8):
            q = q1 * 8 + q0
            value = cell(q)
            unit = (2.0 * (lane + float(q * LANES)) + 1.0) / K - 1.0
            total = total + value * (energy_top * (unit + energy_shift) ** 2)
            f.append(value)
        x0, x1, x2, x3, x4 = real_8(f)
        for n, value in enumerate((x0, x1[0], x1[1], x2[0], x2[1], x3[0], x3[1], x4)):
            stage[q0 * 8 + n] = value
    lattice = lattice_ref[...] + gain_ref[...] * jnp.sum(total, axis=1, keepdims=True)

    def send(u, value):
        n = PLACE[u]
        real, imag = value
        c, s = twist_ref[n, 0:1, :], twist_ref[n, 1:2, :]
        if imag is None:
            real, imag = real * c, real * s
        else:
            real, imag = real * c - imag * s, real * s + imag * c
        for half, part in ((0, real), (1, imag)):
            h, l = split(part)
            place = (slice(n * ROWS, n * ROWS + ROWS), slice(half * LANES, half * LANES + LANES))
            high[place] = h
            low[place] = l

    for u1 in (1, 2, 3):
        x = [(stage[q0 * 8 + 2 * u1 - 1], stage[q0 * 8 + 2 * u1]) for q0 in range(8)]
        x = [x[0]] + [turned(x[q0], 2.0 * np.pi * q0 * u1 / 64) for q0 in range(1, 8)]
        for u0, value in enumerate(complex_8(x)):
            send(u1 + 8 * u0, value)
    for u0, value in enumerate(odd_ahead([stage[q0 * 8 + 7] for q0 in range(8)])):
        send(4 + 8 * u0, value)
    x0, x1, x2, x3, x4 = real_8([stage[q0 * 8] for q0 in range(8)])
    for u, value in ((0, (x0, None)), (8, x1), (16, x2), (24, x3), (32, (x4, None))):
        send(u, value)

    for n in range(0, COUNT, 11):
        rows = slice(n * ROWS, (n + 11) * ROWS)
        spectrum = product(high[rows], low[rows], ahead_ref)
        weight = weight_ref[rows]
        h0, l0 = split(spectrum[:, :LANES] * weight)
        h1, l1 = split(spectrum[:, LANES:] * weight)
        result[rows] = product(
            jnp.concatenate([h0, h1], axis=1), jnp.concatenate([l0, l1], axis=1), back_ref
        )

    def fetch(u):
        n = PLACE[u]
        rows = slice(n * ROWS, n * ROWS + ROWS)
        real, imag = result[rows, :LANES], result[rows, LANES:]
        c, s = twist_ref[n, 0:1, :], twist_ref[n, 1:2, :]
        return imag * c - real * s, real * c + imag * s

    for u1 in (1, 2, 3):
        d = complex_8([fetch(u1 + 8 * u0) for u0 in range(8)])
        for q0 in range(8):
            value = turned(d[q0], 2.0 * np.pi * q0 * u1 / 64) if q0 else d[0]
            stage[q0 * 8 + 2 * u1 - 1] = value[0]
            stage[q0 * 8 + 2 * u1] = value[1]
    for q0, value in enumerate(odd_back([fetch(4 + 8 * u0) for u0 in range(4)])):
        stage[q0 * 8 + 7] = value
    ends = back_8(fetch(0)[0], fetch(8), fetch(16), fetch(24), fetch(32)[0])
    for q0, value in enumerate(ends):
        stage[q0 * 8] = value
    for q0 in range(8):
        d = [stage[q0 * 8 + n] for n in range(8)]
        for q1, value in enumerate(back_8(d[0], (d[1], d[2]), (d[3], d[4]), (d[5], d[6]), d[7])):
            q = q1 * 8 + q0
            m, jb = q // per, q % per
            out_ref[m, jb * ROWS : jb * ROWS + ROWS, :] = value
    lane = lax.broadcasted_iota(jnp.int32, (8, LANES), 1)
    lattice = jnp.where(lane % ROWS < 8, lattice[:8], lattice[8:])
    for m in range(splits):
        out_ref[m, 64:72, :] = lattice


def pack_kernel(first_ref, last_ref, profile_ref, kelvin_ref, up_ref, down_ref, mine_ref):
    profile = profile_ref[pl.ds(lax.axis_index("mom") // (lax.axis_size("mom") // 2), 1), :]
    for out_ref, edge_ref, place in ((up_ref, last_ref, 7), (down_ref, first_ref, 0)):
        for b in range(2):
            row = edge_ref[b, place : place + 1, :]
            for n in range(4):
                out_ref[b * 4 + n : b * 4 + n + 1, :] = row[:, n * LANES : n * LANES + LANES]
        out_ref[8:9, :] = profile
        out_ref[9:10, :] = kelvin_ref[...]
        out_ref[10:16, :] = jnp.zeros((6, LANES), jnp.float32)
    mine_ref[...] = profile


def chosen(area, table_ref):
    value = jnp.zeros(area.shape, jnp.float32)
    for n in range(table_ref.shape[0]):
        value = value + jnp.where(area == n, table_ref[n], 0.0)
    return value


def potential_kernel(quad_ref, four_ref, eight_ref, twelve_ref, below_ref, above_ref, kelvin_ref, area_ref,
                     damping_ref, populace_ref, conductance_ref, weight_ref, lattice_ref, gain_ref,
                     profile, ahead_t, behind_t, ahead_w, behind_w, column):
    spot, mom = lax.axis_index("pos"), lax.axis_index("mom")
    spots = profile.shape[0]
    per_band = lax.axis_size("mom") // 2
    band = (mom // per_band).astype(jnp.float32)
    for k, ref in enumerate((quad_ref, four_ref, eight_ref, twelve_ref)):
        for n, offset in enumerate(QUAD):
            profile[pl.ds((spot + 4 * k + offset + spots) % spots, 1), :] = ref[n : n + 1, :]
    first, last = profile[0:1, 0:1], profile[spots - 1 : spots, LANES - 1 : LANES]
    start = spot * LANES + (mom % per_band) * ROWS
    lead = start // RESIDUES
    inner = pl.multiple_of(start % RESIDUES, 8)
    source = lax.broadcasted_iota(jnp.int32, (spots, LANES), 0)
    lane = lax.broadcasted_iota(jnp.int32, (spots, LANES), 1)
    mirror = (LANES - lane) % LANES
    window = ahead_w.shape[0]
    row_w = lax.broadcasted_iota(jnp.int32, (window, LANES), 0)
    lane_w = lax.broadcasted_iota(jnp.int32, (window, LANES), 1)
    carry = (inner + row_w) // RESIDUES - 1
    ahead_q = lead + carry + lane_w - jnp.where(lane_w >= RESIDUES, LANES, 0)
    behind_q = lead + carry - lane_w + jnp.where(lane_w >= RESIDUES, LANES, 0)
    cells = spots * LANES // RESIDUES

    def pick(place):
        pieces = []
        for h in range(2):
            chooser = jnp.where(place == 2 * source + h, 1.0, 0.0)
            full = lax.dot_general(
                profile[...], chooser, (((0,), (0,)), ((), ())),
                precision=lax.Precision.HIGHEST, preferred_element_type=jnp.float32,
            )
            pieces.append(full[h * RESIDUES : h * RESIDUES + RESIDUES])
        return pieces[0] + pieces[1]

    forward, backward = pick(lane), pick(mirror)
    for n, k in enumerate((-1, 0, 1)):
        rows = slice(n * RESIDUES, n * RESIDUES + RESIDUES)
        ahead_t[rows] = pltpu.roll(forward, (-k) % LANES, 1) if k else forward
        behind_t[rows] = pltpu.roll(backward, k % LANES, 1) if k else backward
    for table, wide, shift, q in (
        (ahead_t, ahead_w, (LANES - lead) % LANES, ahead_q),
        (behind_t, behind_w, lead, behind_q),
    ):
        value = pltpu.roll(table[pl.ds(inner, window), :], shift, 1)
        value = jnp.where(q < 0, first, value)
        wide[...] = jnp.where(q >= cells, last, value)
    for n, u in enumerate(RESIDUE_LIST):
        scale = potential_gain / K * (1.0 if u in (0, 32) else 2.0)
        ahead = ahead_w[RESIDUES + u : RESIDUES + u + ROWS, :]
        behind = behind_w[RESIDUES - u : RESIDUES - u + ROWS, :]
        weight_ref[n * ROWS : n * ROWS + ROWS, :] = scale * (ahead - behind)

    before, after = below_ref[9:10, LANES - 1 : LANES], above_ref[9:10, 0:1]
    column[0:8, :] = jnp.where(spot == 0, 1.0, before) * jnp.ones((8, 1), jnp.float32)
    column[8:136, :] = kelvin_ref[...]
    column[136:144, :] = jnp.where(spot == spots - 1, 1.0, after) * jnp.ones((8, 1), jnp.float32)
    base = pl.multiple_of((mom % per_band) * ROWS, ROWS)
    near = column[pl.ds(base, ROWS + 16), :]
    lower, kelvin, upper = near[7 : 7 + ROWS], near[8 : 8 + ROWS], near[9 : 9 + ROWS]
    area = area_ref[pl.ds(base, ROWS), :]
    relax, dens, cond = chosen(area, damping_ref), chosen(area, populace_ref), chosen(area, conductance_ref)
    lane = lax.broadcasted_iota(jnp.int32, (1, LANES), 1).astype(jnp.float32)
    inverse = -1.0 / kelvin
    total = jnp.zeros((ROWS, LANES), jnp.float32)
    for q in range(RESIDUES):
        unit = (2.0 * (lane + float(q * LANES)) + 1.0) / K - 1.0
        energy = energy_top * (unit + energy_shift) ** 2
        total = total + energy * jnp.exp((energy + band_offset * band) * inverse)
    gain = heat_gain / K * relax
    still = kelvin + cond * (upper - 2.0 * kelvin + lower) - heat_outflow * (kelvin - 1.0)
    lattice_ref[...] = (1.0 - band) * still - gain * dens * jnp.sum(total, axis=1, keepdims=True)
    gain_ref[...] = gain


def local_kernel(grid_ref, below_ref, above_ref, contact_ref, kelvin_ref, area_ref, damping_ref, populace_ref, out_ref):
    spot, mom = lax.axis_index("pos"), lax.axis_index("mom")
    spots = lax.axis_size("pos")
    _, rows, count = grid_ref.shape
    place = lax.broadcasted_iota(jnp.int32, (1, LANES), 1)
    row = lax.broadcasted_iota(jnp.int32, (rows, LANES), 0)
    inverse = -1.0 / kelvin_ref[...]
    relax = chosen(area_ref[...], damping_ref)
    dens = relax * chosen(area_ref[...], populace_ref)
    for n in range(count // LANES):
        lanes = slice(n * LANES, n * LANES + LANES)
        unit = (2.0 * (place + (mom * count + n * LANES)).astype(jnp.float32) + 1.0) / K - 1.0
        velocity = courant * unit
        energy = energy_top * (unit + energy_shift) ** 2
        for b in range(2):
            f = grid_ref[b, :, lanes]
            edge = slice(b * 4 + n, b * 4 + n + 1)
            before = jnp.where(spot == 0, contact_ref[b, 0:1, lanes], below_ref[edge, :])
            after = jnp.where(spot == spots - 1, contact_ref[b, 1:2, lanes], above_ref[edge, :])
            below = jnp.where(row == 0, before, pltpu.roll(f, 1, 0))
            above = jnp.where(row == rows - 1, after, pltpu.roll(f, rows - 1, 0))
            drift = velocity * jnp.where(velocity > 0, below - f, f - above)
            settled = dens * jnp.exp((energy + band_offset * b) * inverse)
            out_ref[b, :, lanes] = f + drift - relax * f + settled


def final_kernel(base_ref, back_ref, out_ref, lattice_ref):
    splits = back_ref.shape[0]
    per_band = splits // 2
    lane = lax.broadcasted_iota(jnp.int32, (8, LANES), 1)
    row = lax.broadcasted_iota(jnp.int32, (8, LANES), 0)
    total = jnp.zeros((8, LANES), jnp.float32)
    for m in range(splits):
        b, first = m // per_band, (m % per_band) * ROWS
        rows = slice(first, first + ROWS)
        for n in range(4):
            lanes = slice(n * LANES, n * LANES + LANES)
            out_ref[b, rows, lanes] = base_ref[b, rows, lanes] + back_ref[m, n * ROWS : n * ROWS + ROWS, :]
        place = lane - first - row
        total = total + jnp.where((place == 0) | (place == 8), back_ref[m, 64:72, :], 0.0)
    lattice_ref[...] = jnp.sum(total, axis=0, keepdims=True)


VM = pl.BlockSpec(memory_space=pltpu.VMEM)
SM = pl.BlockSpec(memory_space=pltpu.SMEM)


def call(kernel, outs, specs, flops=0, moved=0, scratch=(), **more):
    return pl.pallas_call(
        kernel,
        out_shape=outs,
        in_specs=specs,
        out_specs=jax.tree.map(lambda _: VM, outs),
        scratch_shapes=list(scratch),
        compiler_params=pltpu.CompilerParams(vmem_limit_bytes=32 * 2**20),
        cost_estimate=pl.CostEstimate(flops=flops, bytes_accessed=moved, transcendentals=0),
        **more,
    )


def f32(*shape):
    return jax.ShapeDtypeStruct(shape, jnp.float32)


def body(grid, potential, contact, kelvin, area, damping, populace, conductance):
    bands, rows, count = grid.shape
    spots, splits = lax.axis_size("pos"), lax.axis_size("mom")
    ahead, back, twist = tables()

    full = lax.all_to_all(grid.reshape(splits, ROWS, count), "mom", split_axis=0, concat_axis=0)

    def moved(value, offset):
        return lax.ppermute(value, "pos", [((n + offset) % spots, n) for n in range(spots)])

    up, down, mine = pl.pallas_call(
        pack_kernel,
        grid=(1,),
        out_shape=(f32(16, LANES), f32(16, LANES), f32(1, LANES)),
        in_specs=[
            pl.BlockSpec((bands, 8, count), lambda i: (0, 0, 0)),
            pl.BlockSpec((bands, 8, count), lambda i: (0, rows // 8 - 1, 0)),
            pl.BlockSpec((bands, rows), lambda i: (0, 0)),
            pl.BlockSpec((1, rows), lambda i: (0, 0)),
        ],
        out_specs=(
            pl.BlockSpec((16, LANES), lambda i: (0, 0)),
            pl.BlockSpec((16, LANES), lambda i: (0, 0)),
            pl.BlockSpec((1, LANES), lambda i: (0, 0)),
        ),
    )(grid, grid, potential, kelvin.reshape(1, rows))
    below, above, second = moved(up, -1), moved(down, 1), moved(mine, 2)
    quad = jnp.concatenate([mine, below[8:9], above[8:9], second], axis=0)
    far = [moved(quad, 4), moved(quad, 8), moved(quad, 12)]

    kelvin_col, area_col = kelvin.reshape(rows, 1), area.reshape(rows, 1)
    weight, lattice, gain = call(
        potential_kernel,
        (f32(COUNT * ROWS, LANES), f32(ROWS, 1), f32(ROWS, 1)),
        [VM] * 8 + [SM] * 3,
        flops=1000,
        moved=1000,
        scratch=[
            pltpu.VMEM((spots, LANES), jnp.float32),
            pltpu.VMEM((3 * RESIDUES, LANES), jnp.float32),
            pltpu.VMEM((3 * RESIDUES, LANES), jnp.float32),
            pltpu.VMEM((144, LANES), jnp.float32),
            pltpu.VMEM((144, LANES), jnp.float32),
            pltpu.VMEM((144, 1), jnp.float32),
        ],
    )(quad, *far, below, above, kelvin_col, area_col, damping, populace, conductance)
    base = call(
        local_kernel, f32(bands, rows, count), [VM] * 6 + [SM] * 2, flops=1000, moved=1000
    )(grid, below, above, contact, kelvin_col, area_col, damping, populace)

    messages = call(
        transform_kernel,
        f32(splits, FLAT, LANES),
        [VM] * 7,
        flops=10**9,
        moved=2**21,
        scratch=[
            pltpu.VMEM((RESIDUES, ROWS, LANES), jnp.float32),
            pltpu.VMEM((COUNT * ROWS, 2 * LANES), jnp.bfloat16),
            pltpu.VMEM((COUNT * ROWS, 2 * LANES), jnp.bfloat16),
            pltpu.VMEM((COUNT * ROWS, 2 * LANES), jnp.float32),
        ],
    )(full, weight, lattice, gain, jnp.asarray(ahead), jnp.asarray(back), jnp.asarray(twist))
    received = lax.all_to_all(messages, "mom", split_axis=0, concat_axis=0)
    updated, warmth = call(
        final_kernel, (f32(bands, rows, count), f32(1, rows)), [VM, VM], flops=10**6, moved=2**21
    )(base, received)
    return updated, warmth.reshape(rows)


def solution(mesh):
    return jax.shard_map(
        body,
        mesh=mesh,
        in_specs=(
            P(None, "pos", "mom"),
            P(None, "pos"),
            P(None, None, "mom"),
            P("pos"),
            P("pos"),
            P(),
            P(),
            P(),
        ),
        out_specs=(P(None, "pos", "mom"), P("pos")),
        check_vma=False,
    )
```

```python
import functools

import jax
import jax.numpy as jnp
import numpy as np
from jax import lax
from jax.experimental import pallas as pl
from jax.experimental.pallas import tpu as pltpu
from jax.sharding import PartitionSpec as P

K = 8192
LANES = 128
RESIDUES = 64
ROWS = 16
HALF = (0, 1, 4, 5, 8, 9, 12, 13)
FLAT = 72

courant = 0.9
energy_top = 3.0
energy_shift = 0.25
band_offset = 0.5
potential_gain = 0.5
heat_gain = 0.5
heat_outflow = 0.1

RESIDUE_LIST = [u1 + 8 * u0 for u1 in (1, 2, 3) for u0 in range(8)] + [4, 12, 20, 28, 0, 8, 16, 24, 32]
COUNT = len(RESIDUE_LIST)
PLACE = {u: n for n, u in enumerate(RESIDUE_LIST)}
ROOT = float(np.sqrt(0.5))


def tables():
    idx = np.arange(LANES)
    angle = 2.0 * np.pi / LANES * (idx[:, None] * idx[None, :] % LANES)
    cos, sin = np.cos(angle), np.sin(angle)
    ahead = np.block([[cos, sin], [-sin, cos]]).astype(np.float32)

    def parts(matrix):
        high = matrix.astype(jnp.bfloat16)
        low = (matrix - high.astype(np.float32)).astype(jnp.bfloat16)
        return np.stack([high, low])

    turn = 2.0 * np.pi / K * (np.array(RESIDUE_LIST)[:, None] * idx[None, :])
    twist = np.stack([np.cos(turn), np.sin(turn)], axis=1).astype(np.float32)
    return parts(ahead), parts(np.ascontiguousarray(ahead.T)), twist


def add(a, b):
    return (a[0] + b[0], a[1] + b[1])


def sub(a, b):
    return (a[0] - b[0], a[1] - b[1])


def times_i(a):
    return (-a[1], a[0])


def turned(a, angle):
    c, s = float(np.cos(angle)), float(np.sin(angle))
    return (a[0] * c - a[1] * s, a[0] * s + a[1] * c)


def real_8(f):
    a0, a1, b0, b1 = f[0] + f[4], f[0] - f[4], f[2] + f[6], f[2] - f[6]
    c0, c1, d0, d1 = f[1] + f[5], f[1] - f[5], f[3] + f[7], f[3] - f[7]
    even, odd = a0 + b0, c0 + d0
    less, more = ROOT * (c1 - d1), ROOT * (c1 + d1)
    return even + odd, (a1 + less, b1 + more), (a0 - b0, c0 - d0), (a1 - less, more - b1), even - odd


def back_8(x0, d1, d2, d3, x4):
    even, odd = x0 + x4, x0 - x4
    (r1, i1), (r2, i2), (r3, i3) = d1, d2, d3
    ea, eb = even + r2, even - r2
    sr, si = r1 + r3, i3 - i1
    oa, ob = odd - i2, odd + i2
    p, q = ROOT * (r1 - i1), ROOT * (r1 + i1)
    v, w = ROOT * (r3 + i3), ROOT * (r3 - i3)
    pv, wq = p - v, w - q
    return [ea + sr, oa + pv, eb + si, ob + wq, ea - sr, oa - pv, eb - si, ob - wq]


def complex_4(x):
    a, b, c, d = add(x[0], x[2]), sub(x[0], x[2]), add(x[1], x[3]), times_i(sub(x[1], x[3]))
    return [add(a, c), add(b, d), sub(a, c), sub(b, d)]


def complex_8(x):
    e, o = complex_4(x[0::2]), complex_4(x[1::2])
    o[1] = (ROOT * (o[1][0] - o[1][1]), ROOT * (o[1][0] + o[1][1]))
    o[2] = times_i(o[2])
    o[3] = (-ROOT * (o[3][0] + o[3][1]), ROOT * (o[3][0] - o[3][1]))
    return [add(e[n], o[n]) for n in range(4)] + [sub(e[n], o[n]) for n in range(4)]


def cs(n):
    return float(np.cos(np.pi * n / 8)), float(np.sin(np.pi * n / 8))


def odd_ahead(a):
    less = [None] + [a[q] - a[8 - q] for q in (1, 2, 3)]
    more = [None] + [a[q] + a[8 - q] for q in (1, 2, 3)]
    out = [None] * 4
    for u in (0, 1):
        n = 1 + 2 * u
        even_r = a[0] + less[2] * cs(2 * n)[0]
        odd_r = less[1] * cs(n)[0] + less[3] * cs(3 * n)[0]
        even_i = more[2] * cs(2 * n)[1]
        odd_i = more[1] * cs(n)[1] + more[3] * cs(3 * n)[1]
        even_i = even_i + a[4] if u == 0 else even_i - a[4]
        out[u] = (even_r + odd_r, odd_i + even_i)
        out[3 - u] = (even_r - odd_r, odd_i - even_i)
    return out


def odd_back(c):
    (r0, i0), (r1, i1), (r2, i2), (r3, i3) = c
    rp0, rm0, rp1, rm1 = r0 + r3, r0 - r3, r1 + r2, r1 - r2
    ip0, im0, ip1, im1 = i0 + i3, i0 - i3, i1 + i2, i1 - i2
    out = [None] * 8
    out[0] = rp0 + rp1
    out[4] = (i1 + i3) - (i0 + i2)
    for q in (1, 2, 3):
        (c0, s0), (c1, s1) = cs(q), cs(3 * q)
        if q % 2:
            cosines, sines = rm0 * c0 + rm1 * c1, ip0 * s0 + ip1 * s1
        else:
            cosines, sines = rp0 * c0 + rp1 * c1, im0 * s0 + im1 * s1
        out[q], out[8 - q] = cosines - sines, -cosines - sines
    return out


def split(value):
    high = value.astype(jnp.bfloat16)
    return high, (value - high.astype(jnp.float32)).astype(jnp.bfloat16)


def product(high, low, weights):
    dot = functools.partial(jnp.dot, preferred_element_type=jnp.float32)
    return dot(high, weights[0]) + (dot(high, weights[1]) + dot(low, weights[0]))


def transform_kernel(rows_ref, weight_ref, lattice_ref, gain_ref, ahead_ref, back_ref, twist_ref, out_ref,
                     stage, high, low, result):
    splits = rows_ref.shape[0]
    per = RESIDUES // splits

    lane = lax.broadcasted_iota(jnp.int32, (1, LANES), 1).astype(jnp.float32)

    def cell(q):
        n = (q % per) * LANES
        return rows_ref[q // per, :, n : n + LANES]

    total = jnp.zeros((ROWS, LANES), jnp.float32)
    for q0 in range(8):
        f = []
        for q1 in range(8):
            q = q1 * 8 + q0
            value = cell(q)
            unit = (2.0 * (lane + float(q * LANES)) + 1.0) / K - 1.0
            total = total + value * (energy_top * (unit + energy_shift) ** 2)
            f.append(value)
        x0, x1, x2, x3, x4 = real_8(f)
        for n, value in enumerate((x0, x1[0], x1[1], x2[0], x2[1], x3[0], x3[1], x4)):
            stage[q0 * 8 + n] = value
    lattice = lattice_ref[...] + gain_ref[...] * jnp.sum(total, axis=1, keepdims=True)

    def send(u, value):
        n = PLACE[u]
        real, imag = value
        c, s = twist_ref[n, 0:1, :], twist_ref[n, 1:2, :]
        if imag is None:
            real, imag = real * c, real * s
        else:
            real, imag = real * c - imag * s, real * s + imag * c
        for half, part in ((0, real), (1, imag)):
            h, l = split(part)
            place = (slice(n * ROWS, n * ROWS + ROWS), slice(half * LANES, half * LANES + LANES))
            high[place] = h
            low[place] = l

    for u1 in (1, 2, 3):
        x = [(stage[q0 * 8 + 2 * u1 - 1], stage[q0 * 8 + 2 * u1]) for q0 in range(8)]
        x = [x[0]] + [turned(x[q0], 2.0 * np.pi * q0 * u1 / 64) for q0 in range(1, 8)]
        for u0, value in enumerate(complex_8(x)):
            send(u1 + 8 * u0, value)
    for u0, value in enumerate(odd_ahead([stage[q0 * 8 + 7] for q0 in range(8)])):
        send(4 + 8 * u0, value)
    x0, x1, x2, x3, x4 = real_8([stage[q0 * 8] for q0 in range(8)])
    for u, value in ((0, (x0, None)), (8, x1), (16, x2), (24, x3), (32, (x4, None))):
        send(u, value)

    for n in range(0, COUNT, 11):
        rows = slice(n * ROWS, (n + 11) * ROWS)
        spectrum = product(high[rows], low[rows], ahead_ref)
        weight = weight_ref[rows]
        h0, l0 = split(spectrum[:, :LANES] * weight)
        h1, l1 = split(spectrum[:, LANES:] * weight)
        result[rows] = product(
            jnp.concatenate([h0, h1], axis=1), jnp.concatenate([l0, l1], axis=1), back_ref
        )

    def fetch(u):
        n = PLACE[u]
        rows = slice(n * ROWS, n * ROWS + ROWS)
        real, imag = result[rows, :LANES], result[rows, LANES:]
        c, s = twist_ref[n, 0:1, :], twist_ref[n, 1:2, :]
        return imag * c - real * s, real * c + imag * s

    for u1 in (1, 2, 3):
        d = complex_8([fetch(u1 + 8 * u0) for u0 in range(8)])
        for q0 in range(8):
            value = turned(d[q0], 2.0 * np.pi * q0 * u1 / 64) if q0 else d[0]
            stage[q0 * 8 + 2 * u1 - 1] = value[0]
            stage[q0 * 8 + 2 * u1] = value[1]
    for q0, value in enumerate(odd_back([fetch(4 + 8 * u0) for u0 in range(4)])):
        stage[q0 * 8 + 7] = value
    ends = back_8(fetch(0)[0], fetch(8), fetch(16), fetch(24), fetch(32)[0])
    for q0, value in enumerate(ends):
        stage[q0 * 8] = value
    for q0 in range(8):
        d = [stage[q0 * 8 + n] for n in range(8)]
        for q1, value in enumerate(back_8(d[0], (d[1], d[2]), (d[3], d[4]), (d[5], d[6]), d[7])):
            q = q1 * 8 + q0
            m, jb = q // per, q % per
            out_ref[m, jb * ROWS : jb * ROWS + ROWS, :] = value
    lane = lax.broadcasted_iota(jnp.int32, (8, LANES), 1)
    lattice = jnp.where(lane % ROWS < 8, lattice[:8], lattice[8:])
    for m in range(splits):
        out_ref[m, 64:72, :] = lattice


def pack_kernel(first_ref, last_ref, line_ref, profile_ref, near_ref, far_ref):
    even = lax.axis_index("pos") % 2 == 0
    for b in range(2):
        first, last = first_ref[b, 0:1, :], last_ref[b, 7:8, :]
        near, far = jnp.where(even, last, first), jnp.where(even, first, last)
        for n in range(4):
            place, lanes = slice(b * 4 + n, b * 4 + n + 1), slice(n * LANES, n * LANES + LANES)
            near_ref[place, :] = near[:, lanes]
            far_ref[place, :] = far[:, lanes]
    near_ref[8:10, :] = profile_ref[...]
    near_ref[10:11, :] = line_ref[...]
    near_ref[11:16, :] = jnp.zeros((5, LANES), jnp.float32)
    far_ref[8:9, :] = line_ref[...]
    far_ref[9:16, :] = jnp.zeros((7, LANES), jnp.float32)


def column(row, count, first=0):
    lane = lax.broadcasted_iota(jnp.int32, (count, LANES), 1)
    place = lane == lax.broadcasted_iota(jnp.int32, (count, LANES), 0) + first
    return jnp.sum(jnp.where(place, row, 0.0), axis=1, keepdims=True)


def energy_kernel(line_ref, area_ref, damping_ref, populace_ref, after_ref, lattice_ref, gain_ref):
    del after_ref
    mom = lax.axis_index("mom")
    per_band = lax.axis_size("mom") // 2
    band = (mom // per_band).astype(jnp.float32)
    base = (mom % per_band) * ROWS
    inverse = column(-1.0 / line_ref[...], ROWS, base)
    gain = heat_gain / K * column(chosen(area_ref[...], damping_ref), ROWS, base)
    dens = column(chosen(area_ref[...], populace_ref), ROWS, base)
    lane = lax.broadcasted_iota(jnp.int32, (1, LANES), 1).astype(jnp.float32)
    total = jnp.zeros((ROWS, LANES), jnp.float32)
    for q in range(RESIDUES):
        unit = (2.0 * (lane + float(q * LANES)) + 1.0) / K - 1.0
        energy = energy_top * (unit + energy_shift) ** 2
        total = total + energy * jnp.exp((energy + band_offset * band) * inverse)
    lattice_ref[...] = -gain * dens * jnp.sum(total, axis=1, keepdims=True)
    gain_ref[...] = gain


def chosen(area, table_ref):
    value = jnp.zeros(area.shape, jnp.float32)
    for n in range(table_ref.shape[0]):
        value = value + jnp.where(area == n, table_ref[n], 0.0)
    return value


def potential_kernel(half_ref, other_ref, weight_ref, profile, ahead_t, behind_t, ahead_w, behind_w):
    spot, mom = lax.axis_index("pos"), lax.axis_index("mom")
    spots = profile.shape[0]
    per_band = lax.axis_size("mom") // 2
    partner = (spot + jnp.where(spot % 2 == 0, spots - 1, 1)) % spots
    for home, ref in ((spot, half_ref), (partner, other_ref)):
        for n, offset in enumerate(HALF):
            row = jnp.where(mom < per_band, ref[2 * n : 2 * n + 1, :], ref[2 * n + 1 : 2 * n + 2, :])
            profile[pl.ds(home ^ offset, 1), :] = row
    first, last = profile[0:1, 0:1], profile[spots - 1 : spots, LANES - 1 : LANES]
    start = spot * LANES + (mom % per_band) * ROWS
    lead = start // RESIDUES
    inner = pl.multiple_of(start % RESIDUES, 8)
    source = lax.broadcasted_iota(jnp.int32, (spots, LANES), 0)
    lane = lax.broadcasted_iota(jnp.int32, (spots, LANES), 1)
    mirror = (LANES - lane) % LANES
    window = ahead_w.shape[0]
    row_w = lax.broadcasted_iota(jnp.int32, (window, LANES), 0)
    lane_w = lax.broadcasted_iota(jnp.int32, (window, LANES), 1)
    carry = (inner + row_w) // RESIDUES - 1
    ahead_q = lead + carry + lane_w - jnp.where(lane_w >= RESIDUES, LANES, 0)
    behind_q = lead + carry - lane_w + jnp.where(lane_w >= RESIDUES, LANES, 0)
    cells = spots * LANES // RESIDUES

    def pick(place):
        pieces = []
        for h in range(2):
            chooser = jnp.where(place == 2 * source + h, 1.0, 0.0)
            full = lax.dot_general(
                profile[...], chooser, (((0,), (0,)), ((), ())),
                precision=lax.Precision.HIGHEST, preferred_element_type=jnp.float32,
            )
            pieces.append(full[h * RESIDUES : h * RESIDUES + RESIDUES])
        return pieces[0] + pieces[1]

    forward, backward = pick(lane), pick(mirror)
    for n, k in enumerate((-1, 0, 1)):
        rows = slice(n * RESIDUES, n * RESIDUES + RESIDUES)
        ahead_t[rows] = pltpu.roll(forward, (-k) % LANES, 1) if k else forward
        behind_t[rows] = pltpu.roll(backward, k % LANES, 1) if k else backward
    for table, wide, shift, q in (
        (ahead_t, ahead_w, (LANES - lead) % LANES, ahead_q),
        (behind_t, behind_w, lead, behind_q),
    ):
        value = pltpu.roll(table[pl.ds(inner, window), :], shift, 1)
        value = jnp.where(q < 0, first, value)
        wide[...] = jnp.where(q >= cells, last, value)
    for n, u in enumerate(RESIDUE_LIST):
        scale = potential_gain / K * (1.0 if u in (0, 32) else 2.0)
        ahead = ahead_w[RESIDUES + u : RESIDUES + u + ROWS, :]
        behind = behind_w[RESIDUES - u : RESIDUES - u + ROWS, :]
        weight_ref[n * ROWS : n * ROWS + ROWS, :] = scale * (ahead - behind)


def local_kernel(grid_ref, near_ref, far_ref, contact_ref, line_ref, area_ref, damping_ref, populace_ref,
                 conductance_ref, after_ref, out_ref, still_ref):
    del after_ref
    spot, mom = lax.axis_index("pos"), lax.axis_index("mom")
    spots = lax.axis_size("pos")
    even = spot % 2 == 0
    _, rows, count = grid_ref.shape
    place = lax.broadcasted_iota(jnp.int32, (1, LANES), 1)
    row = lax.broadcasted_iota(jnp.int32, (rows, LANES), 0)
    kelvin, area = line_ref[...], area_ref[...]
    inverse = column(-1.0 / kelvin, rows)
    relax = column(chosen(area, damping_ref), rows)
    dens = column(chosen(area, populace_ref), rows)
    for n in range(count // LANES):
        lanes = slice(n * LANES, n * LANES + LANES)
        unit = (2.0 * (place + (mom * count + n * LANES)).astype(jnp.float32) + 1.0) / K - 1.0
        velocity = courant * unit
        energy = energy_top * (unit + energy_shift) ** 2
        for b in range(2):
            f = grid_ref[b, :, lanes]
            edge = b * 4 + n
            near, far = near_ref[edge : edge + 1, :], far_ref[16 + edge : 17 + edge, :]
            before = jnp.where(spot == 0, contact_ref[b, 0:1, lanes], jnp.where(even, far, near))
            after = jnp.where(spot == spots - 1, contact_ref[b, 1:2, lanes], jnp.where(even, near, far))
            below = jnp.where(row == 0, before, pltpu.roll(f, 1, 0))
            above = jnp.where(row == rows - 1, after, pltpu.roll(f, rows - 1, 0))
            drift = velocity * jnp.where(velocity > 0, below - f, f - above)
            excess = f - dens * jnp.exp((energy + band_offset * b) * inverse)
            out_ref[b, :, lanes] = f + drift - relax * excess

    near, far = near_ref[10:11, :], far_ref[24:25, :]
    below = jnp.where(spot == 0, 1.0, jnp.where(even, far, near)[:, LANES - 1 : LANES])
    above = jnp.where(spot == spots - 1, 1.0, jnp.where(even, near, far)[:, 0:1])
    lower = jnp.where(place == 0, below, pltpu.roll(kelvin, 1, 1))
    upper = jnp.where(place == LANES - 1, above, pltpu.roll(kelvin, LANES - 1, 1))
    flow = chosen(area, conductance_ref) * (upper - 2.0 * kelvin + lower)
    still_ref[...] = kelvin + flow - heat_outflow * (kelvin - 1.0)


def final_kernel(base_ref, back_ref, still_ref, out_ref, lattice_ref):
    splits = back_ref.shape[0]
    per_band = splits // 2
    lane = lax.broadcasted_iota(jnp.int32, (8, LANES), 1)
    row = lax.broadcasted_iota(jnp.int32, (8, LANES), 0)
    total = jnp.zeros((8, LANES), jnp.float32)
    for m in range(splits):
        b, first = m // per_band, (m % per_band) * ROWS
        rows = slice(first, first + ROWS)
        for n in range(4):
            lanes = slice(n * LANES, n * LANES + LANES)
            out_ref[b, rows, lanes] = base_ref[b, rows, lanes] + back_ref[m, n * ROWS : n * ROWS + ROWS, :]
        place = lane - first - row
        total = total + jnp.where((place == 0) | (place == 8), back_ref[m, 64:72, :], 0.0)
    lattice_ref[...] = still_ref[...] + jnp.sum(total, axis=0, keepdims=True)


VM = pl.BlockSpec(memory_space=pltpu.VMEM)
SM = pl.BlockSpec(memory_space=pltpu.SMEM)


def call(kernel, outs, specs, flops=0, moved=0, scratch=(), **more):
    return pl.pallas_call(
        kernel,
        out_shape=outs,
        in_specs=specs,
        out_specs=jax.tree.map(lambda _: VM, outs),
        scratch_shapes=list(scratch),
        compiler_params=pltpu.CompilerParams(vmem_limit_bytes=32 * 2**20),
        cost_estimate=pl.CostEstimate(flops=flops, bytes_accessed=moved, transcendentals=0),
        **more,
    )


def f32(*shape):
    return jax.ShapeDtypeStruct(shape, jnp.float32)


def body(grid, potential, contact, kelvin, area, damping, populace, conductance):
    bands, rows, count = grid.shape
    spots, splits = lax.axis_size("pos"), lax.axis_size("mom")
    ahead, back, twist = tables()

    def swapped(value, mask):
        return lax.ppermute(value, "pos", [(n ^ mask, n) for n in range(spots)])

    full = lax.all_to_all(grid.reshape(splits, ROWS, count), "mom", split_axis=0, concat_axis=0)
    kelvin_row, area_row = kelvin.reshape(1, rows), area.reshape(1, rows)
    message = pl.BlockSpec((16, LANES), lambda i: (0, 0))
    core, outer = pl.pallas_call(
        pack_kernel,
        grid=(1,),
        out_shape=(f32(16, LANES), f32(16, LANES)),
        in_specs=[
            pl.BlockSpec((bands, 8, count), lambda i: (0, 0, 0)),
            pl.BlockSpec((bands, 8, count), lambda i: (0, rows // 8 - 1, 0)),
            pl.BlockSpec((1, rows), lambda i: (0, 0)),
            pl.BlockSpec((bands, rows), lambda i: (0, 0)),
        ],
        out_specs=(message, message),
        cost_estimate=pl.CostEstimate(flops=1000, bytes_accessed=1000, transcendentals=0),
    )(grid, grid, kelvin_row, potential)
    near = swapped(core, 1)
    pair = jnp.concatenate([core[8:10], near[8:10]], axis=0)
    outer = jnp.concatenate([pair, swapped(pair, 4), swapped(pair, 8), swapped(pair, 12), outer], axis=0)
    far = lax.ppermute(outer, "pos", [((n + (1 if n % 2 else -1)) % spots, n) for n in range(spots)])

    weight = call(
        potential_kernel,
        f32(COUNT * ROWS, LANES),
        [VM] * 2,
        flops=1000,
        moved=1000,
        scratch=[
            pltpu.VMEM((spots, LANES), jnp.float32),
            pltpu.VMEM((3 * RESIDUES, LANES), jnp.float32),
            pltpu.VMEM((3 * RESIDUES, LANES), jnp.float32),
            pltpu.VMEM((144, LANES), jnp.float32),
            pltpu.VMEM((144, LANES), jnp.float32),
        ],
    )(outer, far)
    lattice, gain = call(
        energy_kernel,
        (f32(ROWS, 1), f32(ROWS, 1)),
        [VM] * 2 + [SM] * 2 + [pl.BlockSpec(memory_space=pl.ANY)],
        flops=1000,
        moved=1000,
    )(kelvin_row, area_row, damping, populace, outer)
    messages = call(
        transform_kernel,
        f32(splits, FLAT, LANES),
        [VM] * 7,
        flops=10**9,
        moved=2**21,
        scratch=[
            pltpu.VMEM((RESIDUES, ROWS, LANES), jnp.float32),
            pltpu.VMEM((COUNT * ROWS, 2 * LANES), jnp.bfloat16),
            pltpu.VMEM((COUNT * ROWS, 2 * LANES), jnp.bfloat16),
            pltpu.VMEM((COUNT * ROWS, 2 * LANES), jnp.float32),
        ],
    )(full, weight, lattice, gain, jnp.asarray(ahead), jnp.asarray(back), jnp.asarray(twist))
    received = lax.all_to_all(messages, "mom", split_axis=0, concat_axis=0)

    base, still = call(
        local_kernel,
        (f32(bands, rows, count), f32(1, rows)),
        [VM] * 6 + [SM] * 3 + [pl.BlockSpec(memory_space=pl.ANY)],
        flops=1000,
        moved=1000,
    )(grid, near, far, contact, kelvin_row, area_row, damping, populace, conductance, messages)
    updated, warmth = call(
        final_kernel, (f32(bands, rows, count), f32(1, rows)), [VM] * 3, flops=10**6, moved=2**21
    )(base, received, still)
    return updated, warmth.reshape(rows)


def solution(mesh):
    return jax.shard_map(
        body,
        mesh=mesh,
        in_specs=(
            P(None, "pos", "mom"),
            P(None, "pos"),
            P(None, None, "mom"),
            P("pos"),
            P("pos"),
            P(),
            P(),
            P(),
        ),
        out_specs=(P(None, "pos", "mom"), P("pos")),
        check_vma=False,
    )
```

```python
import functools

import jax
import jax.numpy as jnp
import numpy as np
from jax import lax
from jax.experimental import pallas as pl
from jax.experimental.pallas import tpu as pltpu
from jax.sharding import PartitionSpec as P

K = 8192
LANES = 128
RESIDUES = 64
ROWS = 16
ORDER = [7, 2, 14, 8, 13, 11, 15, 9, 10, 5, 6, 1, 0, 3, 4, 12]
HALF = (0, 1, 4, 5, 8, 9, 12, 13)
FLAT = 72

courant = 0.9
energy_top = 3.0
energy_shift = 0.25
band_offset = 0.5
potential_gain = 0.5
heat_gain = 0.5
heat_outflow = 0.1

RESIDUE_LIST = [u1 + 8 * u0 for u1 in (1, 2, 3) for u0 in range(8)] + [4, 12, 20, 28, 0, 8, 16, 24, 32]
COUNT = len(RESIDUE_LIST)
PLACE = {u: n for n, u in enumerate(RESIDUE_LIST)}
ROOT = float(np.sqrt(0.5))


def tables():
    idx = np.arange(LANES)
    angle = 2.0 * np.pi / LANES * (idx[:, None] * idx[None, :] % LANES)
    cos, sin = np.cos(angle), np.sin(angle)
    ahead = np.block([[cos, sin], [-sin, cos]]).astype(np.float32)

    def parts(matrix):
        high = matrix.astype(jnp.bfloat16)
        low = (matrix - high.astype(np.float32)).astype(jnp.bfloat16)
        return np.stack([high, low])

    turn = 2.0 * np.pi / K * (np.array(RESIDUE_LIST)[:, None] * idx[None, :])
    twist = np.stack([np.cos(turn), np.sin(turn)], axis=1).astype(np.float32)
    return parts(ahead), parts(np.ascontiguousarray(ahead.T)), twist


def owner_number():
    mom, rank = lax.axis_index("mom"), 0
    for n, device in enumerate(ORDER):
        rank = rank + jnp.where(mom == device, n, 0)
    return rank


def add(a, b):
    return (a[0] + b[0], a[1] + b[1])


def sub(a, b):
    return (a[0] - b[0], a[1] - b[1])


def times_i(a):
    return (-a[1], a[0])


def turned(a, angle):
    c, s = float(np.cos(angle)), float(np.sin(angle))
    return (a[0] * c - a[1] * s, a[0] * s + a[1] * c)


def real_8(f):
    a0, a1, b0, b1 = f[0] + f[4], f[0] - f[4], f[2] + f[6], f[2] - f[6]
    c0, c1, d0, d1 = f[1] + f[5], f[1] - f[5], f[3] + f[7], f[3] - f[7]
    even, odd = a0 + b0, c0 + d0
    less, more = ROOT * (c1 - d1), ROOT * (c1 + d1)
    return even + odd, (a1 + less, b1 + more), (a0 - b0, c0 - d0), (a1 - less, more - b1), even - odd


def back_8(x0, d1, d2, d3, x4):
    even, odd = x0 + x4, x0 - x4
    (r1, i1), (r2, i2), (r3, i3) = d1, d2, d3
    ea, eb = even + r2, even - r2
    sr, si = r1 + r3, i3 - i1
    oa, ob = odd - i2, odd + i2
    p, q = ROOT * (r1 - i1), ROOT * (r1 + i1)
    v, w = ROOT * (r3 + i3), ROOT * (r3 - i3)
    pv, wq = p - v, w - q
    return [ea + sr, oa + pv, eb + si, ob + wq, ea - sr, oa - pv, eb - si, ob - wq]


def complex_4(x):
    a, b, c, d = add(x[0], x[2]), sub(x[0], x[2]), add(x[1], x[3]), times_i(sub(x[1], x[3]))
    return [add(a, c), add(b, d), sub(a, c), sub(b, d)]


def complex_8(x):
    e, o = complex_4(x[0::2]), complex_4(x[1::2])
    o[1] = (ROOT * (o[1][0] - o[1][1]), ROOT * (o[1][0] + o[1][1]))
    o[2] = times_i(o[2])
    o[3] = (-ROOT * (o[3][0] + o[3][1]), ROOT * (o[3][0] - o[3][1]))
    return [add(e[n], o[n]) for n in range(4)] + [sub(e[n], o[n]) for n in range(4)]


def cs(n):
    return float(np.cos(np.pi * n / 8)), float(np.sin(np.pi * n / 8))


def odd_ahead(a):
    less = [None] + [a[q] - a[8 - q] for q in (1, 2, 3)]
    more = [None] + [a[q] + a[8 - q] for q in (1, 2, 3)]
    out = [None] * 4
    for u in (0, 1):
        n = 1 + 2 * u
        even_r = a[0] + less[2] * cs(2 * n)[0]
        odd_r = less[1] * cs(n)[0] + less[3] * cs(3 * n)[0]
        even_i = more[2] * cs(2 * n)[1]
        odd_i = more[1] * cs(n)[1] + more[3] * cs(3 * n)[1]
        even_i = even_i + a[4] if u == 0 else even_i - a[4]
        out[u] = (even_r + odd_r, odd_i + even_i)
        out[3 - u] = (even_r - odd_r, odd_i - even_i)
    return out


def odd_back(c):
    (r0, i0), (r1, i1), (r2, i2), (r3, i3) = c
    rp0, rm0, rp1, rm1 = r0 + r3, r0 - r3, r1 + r2, r1 - r2
    ip0, im0, ip1, im1 = i0 + i3, i0 - i3, i1 + i2, i1 - i2
    out = [None] * 8
    out[0] = rp0 + rp1
    out[4] = (i1 + i3) - (i0 + i2)
    for q in (1, 2, 3):
        (c0, s0), (c1, s1) = cs(q), cs(3 * q)
        if q % 2:
            cosines, sines = rm0 * c0 + rm1 * c1, ip0 * s0 + ip1 * s1
        else:
            cosines, sines = rp0 * c0 + rp1 * c1, im0 * s0 + im1 * s1
        out[q], out[8 - q] = cosines - sines, -cosines - sines
    return out


def split(value):
    high = value.astype(jnp.bfloat16)
    return high, (value - high.astype(jnp.float32)).astype(jnp.bfloat16)


def product(high, low, weights):
    dot = functools.partial(jnp.dot, preferred_element_type=jnp.float32)
    return dot(high, weights[0]) + (dot(high, weights[1]) + dot(low, weights[0]))


def transform_kernel(rows_ref, weight_ref, lattice_ref, gain_ref, ahead_ref, back_ref, twist_ref, out_ref,
                     stage, high, low, result):
    splits = rows_ref.shape[0]
    per = RESIDUES // splits

    lane = lax.broadcasted_iota(jnp.int32, (1, LANES), 1).astype(jnp.float32)

    def cell(q):
        n = (q % per) * LANES
        return rows_ref[ORDER.index(q // per), :, n : n + LANES]

    total = jnp.zeros((ROWS, LANES), jnp.float32)
    for q0 in range(8):
        f = []
        for q1 in range(8):
            q = q1 * 8 + q0
            value = cell(q)
            unit = (2.0 * (lane + float(q * LANES)) + 1.0) / K - 1.0
            total = total + value * (energy_top * (unit + energy_shift) ** 2)
            f.append(value)
        x0, x1, x2, x3, x4 = real_8(f)
        for n, value in enumerate((x0, x1[0], x1[1], x2[0], x2[1], x3[0], x3[1], x4)):
            stage[q0 * 8 + n] = value
    lattice = lattice_ref[...] + gain_ref[...] * jnp.sum(total, axis=1, keepdims=True)

    def send(u, value):
        n = PLACE[u]
        real, imag = value
        c, s = twist_ref[n, 0:1, :], twist_ref[n, 1:2, :]
        if imag is None:
            real, imag = real * c, real * s
        else:
            real, imag = real * c - imag * s, real * s + imag * c
        for half, part in ((0, real), (1, imag)):
            h, l = split(part)
            place = (slice(n * ROWS, n * ROWS + ROWS), slice(half * LANES, half * LANES + LANES))
            high[place] = h
            low[place] = l

    for u1 in (1, 2, 3):
        x = [(stage[q0 * 8 + 2 * u1 - 1], stage[q0 * 8 + 2 * u1]) for q0 in range(8)]
        x = [x[0]] + [turned(x[q0], 2.0 * np.pi * q0 * u1 / 64) for q0 in range(1, 8)]
        for u0, value in enumerate(complex_8(x)):
            send(u1 + 8 * u0, value)
    for u0, value in enumerate(odd_ahead([stage[q0 * 8 + 7] for q0 in range(8)])):
        send(4 + 8 * u0, value)
    x0, x1, x2, x3, x4 = real_8([stage[q0 * 8] for q0 in range(8)])
    for u, value in ((0, (x0, None)), (8, x1), (16, x2), (24, x3), (32, (x4, None))):
        send(u, value)

    for n in range(0, COUNT, 11):
        rows = slice(n * ROWS, (n + 11) * ROWS)
        spectrum = product(high[rows], low[rows], ahead_ref)
        weight = weight_ref[rows]
        h0, l0 = split(spectrum[:, :LANES] * weight)
        h1, l1 = split(spectrum[:, LANES:] * weight)
        result[rows] = product(
            jnp.concatenate([h0, h1], axis=1), jnp.concatenate([l0, l1], axis=1), back_ref
        )

    def fetch(u):
        n = PLACE[u]
        rows = slice(n * ROWS, n * ROWS + ROWS)
        real, imag = result[rows, :LANES], result[rows, LANES:]
        c, s = twist_ref[n, 0:1, :], twist_ref[n, 1:2, :]
        return imag * c - real * s, real * c + imag * s

    for u1 in (1, 2, 3):
        d = complex_8([fetch(u1 + 8 * u0) for u0 in range(8)])
        for q0 in range(8):
            value = turned(d[q0], 2.0 * np.pi * q0 * u1 / 64) if q0 else d[0]
            stage[q0 * 8 + 2 * u1 - 1] = value[0]
            stage[q0 * 8 + 2 * u1] = value[1]
    for q0, value in enumerate(odd_back([fetch(4 + 8 * u0) for u0 in range(4)])):
        stage[q0 * 8 + 7] = value
    ends = back_8(fetch(0)[0], fetch(8), fetch(16), fetch(24), fetch(32)[0])
    for q0, value in enumerate(ends):
        stage[q0 * 8] = value
    for q0 in range(8):
        d = [stage[q0 * 8 + n] for n in range(8)]
        for q1, value in enumerate(back_8(d[0], (d[1], d[2]), (d[3], d[4]), (d[5], d[6]), d[7])):
            q = q1 * 8 + q0
            m, jb = ORDER.index(q // per), q % per
            out_ref[m, jb * ROWS : jb * ROWS + ROWS, :] = value
    lane = lax.broadcasted_iota(jnp.int32, (8, LANES), 1)
    lattice = jnp.where(lane % ROWS < 8, lattice[:8], lattice[8:])
    for m in range(splits):
        out_ref[m, 64:72, :] = lattice


def pack_kernel(first_ref, last_ref, line_ref, profile_ref, near_ref, far_ref):
    even = lax.axis_index("pos") % 2 == 0
    for b in range(2):
        first, last = first_ref[b, 0:1, :], last_ref[b, 7:8, :]
        near, far = jnp.where(even, last, first), jnp.where(even, first, last)
        for n in range(4):
            place, lanes = slice(b * 4 + n, b * 4 + n + 1), slice(n * LANES, n * LANES + LANES)
            near_ref[place, :] = near[:, lanes]
            far_ref[place, :] = far[:, lanes]
    near_ref[8:10, :] = profile_ref[...]
    near_ref[10:11, :] = line_ref[...]
    near_ref[11:16, :] = jnp.zeros((5, LANES), jnp.float32)
    far_ref[8:9, :] = line_ref[...]
    far_ref[9:16, :] = jnp.zeros((7, LANES), jnp.float32)


def column(row, count, first=0):
    lane = lax.broadcasted_iota(jnp.int32, (count, LANES), 1)
    place = lane == lax.broadcasted_iota(jnp.int32, (count, LANES), 0) + first
    return jnp.sum(jnp.where(place, row, 0.0), axis=1, keepdims=True)


def energy_kernel(line_ref, area_ref, damping_ref, populace_ref, after_ref, lattice_ref, gain_ref):
    del after_ref
    owner = owner_number()
    per_band = lax.axis_size("mom") // 2
    band = (owner // per_band).astype(jnp.float32)
    base = (owner % per_band) * ROWS
    inverse = column(-1.0 / line_ref[...], ROWS, base)
    gain = heat_gain / K * column(chosen(area_ref[...], damping_ref), ROWS, base)
    dens = column(chosen(area_ref[...], populace_ref), ROWS, base)
    lane = lax.broadcasted_iota(jnp.int32, (1, LANES), 1).astype(jnp.float32)
    total = jnp.zeros((ROWS, LANES), jnp.float32)
    for q in range(RESIDUES):
        unit = (2.0 * (lane + float(q * LANES)) + 1.0) / K - 1.0
        energy = energy_top * (unit + energy_shift) ** 2
        total = total + energy * jnp.exp((energy + band_offset * band) * inverse)
    lattice_ref[...] = -gain * dens * jnp.sum(total, axis=1, keepdims=True)
    gain_ref[...] = gain


def chosen(area, table_ref):
    value = jnp.zeros(area.shape, jnp.float32)
    for n in range(table_ref.shape[0]):
        value = value + jnp.where(area == n, table_ref[n], 0.0)
    return value


def potential_kernel(half_ref, other_ref, weight_ref, profile, ahead_t, behind_t, ahead_w, behind_w):
    spot, owner = lax.axis_index("pos"), owner_number()
    spots = profile.shape[0]
    per_band = lax.axis_size("mom") // 2
    partner = (spot + jnp.where(spot % 2 == 0, spots - 1, 1)) % spots
    for home, ref in ((spot, half_ref), (partner, other_ref)):
        for n, offset in enumerate(HALF):
            row = jnp.where(owner < per_band, ref[2 * n : 2 * n + 1, :], ref[2 * n + 1 : 2 * n + 2, :])
            profile[pl.ds(home ^ offset, 1), :] = row
    first, last = profile[0:1, 0:1], profile[spots - 1 : spots, LANES - 1 : LANES]
    start = spot * LANES + (owner % per_band) * ROWS
    lead = start // RESIDUES
    inner = pl.multiple_of(start % RESIDUES, 8)
    source = lax.broadcasted_iota(jnp.int32, (spots, LANES), 0)
    lane = lax.broadcasted_iota(jnp.int32, (spots, LANES), 1)
    mirror = (LANES - lane) % LANES
    window = ahead_w.shape[0]
    row_w = lax.broadcasted_iota(jnp.int32, (window, LANES), 0)
    lane_w = lax.broadcasted_iota(jnp.int32, (window, LANES), 1)
    carry = (inner + row_w) // RESIDUES - 1
    ahead_q = lead + carry + lane_w - jnp.where(lane_w >= RESIDUES, LANES, 0)
    behind_q = lead + carry - lane_w + jnp.where(lane_w >= RESIDUES, LANES, 0)
    cells = spots * LANES // RESIDUES

    def pick(place):
        pieces = []
        for h in range(2):
            chooser = jnp.where(place == 2 * source + h, 1.0, 0.0)
            full = lax.dot_general(
                profile[...], chooser, (((0,), (0,)), ((), ())),
                precision=lax.Precision.HIGHEST, preferred_element_type=jnp.float32,
            )
            pieces.append(full[h * RESIDUES : h * RESIDUES + RESIDUES])
        return pieces[0] + pieces[1]

    forward, backward = pick(lane), pick(mirror)
    for n, k in enumerate((-1, 0, 1)):
        rows = slice(n * RESIDUES, n * RESIDUES + RESIDUES)
        ahead_t[rows] = pltpu.roll(forward, (-k) % LANES, 1) if k else forward
        behind_t[rows] = pltpu.roll(backward, k % LANES, 1) if k else backward
    for table, wide, shift, q in (
        (ahead_t, ahead_w, (LANES - lead) % LANES, ahead_q),
        (behind_t, behind_w, lead, behind_q),
    ):
        value = pltpu.roll(table[pl.ds(inner, window), :], shift, 1)
        value = jnp.where(q < 0, first, value)
        wide[...] = jnp.where(q >= cells, last, value)
    for n, u in enumerate(RESIDUE_LIST):
        scale = potential_gain / K * (1.0 if u in (0, 32) else 2.0)
        ahead = ahead_w[RESIDUES + u : RESIDUES + u + ROWS, :]
        behind = behind_w[RESIDUES - u : RESIDUES - u + ROWS, :]
        weight_ref[n * ROWS : n * ROWS + ROWS, :] = scale * (ahead - behind)


def local_kernel(grid_ref, near_ref, far_ref, contact_ref, line_ref, area_ref, damping_ref, populace_ref,
                 conductance_ref, after_ref, out_ref, still_ref):
    del after_ref
    spot, mom = lax.axis_index("pos"), lax.axis_index("mom")
    spots = lax.axis_size("pos")
    even = spot % 2 == 0
    _, rows, count = grid_ref.shape
    place = lax.broadcasted_iota(jnp.int32, (1, LANES), 1)
    row = lax.broadcasted_iota(jnp.int32, (rows, LANES), 0)
    kelvin, area = line_ref[...], area_ref[...]
    inverse = column(-1.0 / kelvin, rows)
    relax = column(chosen(area, damping_ref), rows)
    dens = column(chosen(area, populace_ref), rows)
    for n in range(count // LANES):
        lanes = slice(n * LANES, n * LANES + LANES)
        unit = (2.0 * (place + (mom * count + n * LANES)).astype(jnp.float32) + 1.0) / K - 1.0
        velocity = courant * unit
        energy = energy_top * (unit + energy_shift) ** 2
        for b in range(2):
            f = grid_ref[b, :, lanes]
            edge = b * 4 + n
            near, far = near_ref[edge : edge + 1, :], far_ref[16 + edge : 17 + edge, :]
            before = jnp.where(spot == 0, contact_ref[b, 0:1, lanes], jnp.where(even, far, near))
            after = jnp.where(spot == spots - 1, contact_ref[b, 1:2, lanes], jnp.where(even, near, far))
            below = jnp.where(row == 0, before, pltpu.roll(f, 1, 0))
            above = jnp.where(row == rows - 1, after, pltpu.roll(f, rows - 1, 0))
            drift = velocity * jnp.where(velocity > 0, below - f, f - above)
            excess = f - dens * jnp.exp((energy + band_offset * b) * inverse)
            out_ref[b, :, lanes] = f + drift - relax * excess

    near, far = near_ref[10:11, :], far_ref[24:25, :]
    below = jnp.where(spot == 0, 1.0, jnp.where(even, far, near)[:, LANES - 1 : LANES])
    above = jnp.where(spot == spots - 1, 1.0, jnp.where(even, near, far)[:, 0:1])
    lower = jnp.where(place == 0, below, pltpu.roll(kelvin, 1, 1))
    upper = jnp.where(place == LANES - 1, above, pltpu.roll(kelvin, LANES - 1, 1))
    flow = chosen(area, conductance_ref) * (upper - 2.0 * kelvin + lower)
    still_ref[...] = kelvin + flow - heat_outflow * (kelvin - 1.0)


def final_kernel(base_ref, back_ref, still_ref, out_ref, lattice_ref):
    splits = back_ref.shape[0]
    per_band = splits // 2
    lane = lax.broadcasted_iota(jnp.int32, (8, LANES), 1)
    row = lax.broadcasted_iota(jnp.int32, (8, LANES), 0)
    total = jnp.zeros((8, LANES), jnp.float32)
    for m in range(splits):
        b, first = m // per_band, (m % per_band) * ROWS
        rows = slice(first, first + ROWS)
        for n in range(4):
            lanes = slice(n * LANES, n * LANES + LANES)
            out_ref[b, rows, lanes] = base_ref[b, rows, lanes] + back_ref[m, n * ROWS : n * ROWS + ROWS, :]
        place = lane - first - row
        total = total + jnp.where((place == 0) | (place == 8), back_ref[m, 64:72, :], 0.0)
    lattice_ref[...] = still_ref[...] + jnp.sum(total, axis=0, keepdims=True)


VM = pl.BlockSpec(memory_space=pltpu.VMEM)
SM = pl.BlockSpec(memory_space=pltpu.SMEM)


def call(kernel, outs, specs, flops=0, moved=0, scratch=(), **more):
    return pl.pallas_call(
        kernel,
        out_shape=outs,
        in_specs=specs,
        out_specs=jax.tree.map(lambda _: VM, outs),
        scratch_shapes=list(scratch),
        compiler_params=pltpu.CompilerParams(vmem_limit_bytes=32 * 2**20),
        cost_estimate=pl.CostEstimate(flops=flops, bytes_accessed=moved, transcendentals=0),
        **more,
    )


def f32(*shape):
    return jax.ShapeDtypeStruct(shape, jnp.float32)


def body(grid, potential, contact, kelvin, area, damping, populace, conductance):
    bands, rows, count = grid.shape
    spots, splits = lax.axis_size("pos"), lax.axis_size("mom")
    ahead, back, twist = tables()

    def swapped(value, mask):
        return lax.ppermute(value, "pos", [(n ^ mask, n) for n in range(spots)])

    def exchanged(value):
        return lax.all_to_all(value, "mom", split_axis=0, concat_axis=0, axis_index_groups=[ORDER])

    full = exchanged(grid.reshape(splits, ROWS, count))
    kelvin_row, area_row = kelvin.reshape(1, rows), area.reshape(1, rows)
    message = pl.BlockSpec((16, LANES), lambda i: (0, 0))
    core, outer = pl.pallas_call(
        pack_kernel,
        grid=(1,),
        out_shape=(f32(16, LANES), f32(16, LANES)),
        in_specs=[
            pl.BlockSpec((bands, 8, count), lambda i: (0, 0, 0)),
            pl.BlockSpec((bands, 8, count), lambda i: (0, rows // 8 - 1, 0)),
            pl.BlockSpec((1, rows), lambda i: (0, 0)),
            pl.BlockSpec((bands, rows), lambda i: (0, 0)),
        ],
        out_specs=(message, message),
        cost_estimate=pl.CostEstimate(flops=1000, bytes_accessed=1000, transcendentals=0),
    )(grid, grid, kelvin_row, potential)
    near = swapped(core, 1)
    pair = jnp.concatenate([core[8:10], near[8:10]], axis=0)
    outer = jnp.concatenate([pair, swapped(pair, 4), swapped(pair, 8), swapped(pair, 12), outer], axis=0)
    far = lax.ppermute(outer, "pos", [((n + (1 if n % 2 else -1)) % spots, n) for n in range(spots)])

    weight = call(
        potential_kernel,
        f32(COUNT * ROWS, LANES),
        [VM] * 2,
        flops=1000,
        moved=1000,
        scratch=[
            pltpu.VMEM((spots, LANES), jnp.float32),
            pltpu.VMEM((3 * RESIDUES, LANES), jnp.float32),
            pltpu.VMEM((3 * RESIDUES, LANES), jnp.float32),
            pltpu.VMEM((144, LANES), jnp.float32),
            pltpu.VMEM((144, LANES), jnp.float32),
        ],
    )(outer, far)
    lattice, gain = call(
        energy_kernel,
        (f32(ROWS, 1), f32(ROWS, 1)),
        [VM] * 2 + [SM] * 2 + [pl.BlockSpec(memory_space=pl.ANY)],
        flops=1000,
        moved=1000,
    )(kelvin_row, area_row, damping, populace, outer)
    messages = call(
        transform_kernel,
        f32(splits, FLAT, LANES),
        [VM] * 7,
        flops=10**9,
        moved=2**21,
        scratch=[
            pltpu.VMEM((RESIDUES, ROWS, LANES), jnp.float32),
            pltpu.VMEM((COUNT * ROWS, 2 * LANES), jnp.bfloat16),
            pltpu.VMEM((COUNT * ROWS, 2 * LANES), jnp.bfloat16),
            pltpu.VMEM((COUNT * ROWS, 2 * LANES), jnp.float32),
        ],
    )(full, weight, lattice, gain, jnp.asarray(ahead), jnp.asarray(back), jnp.asarray(twist))
    received = exchanged(messages)

    base, still = call(
        local_kernel,
        (f32(bands, rows, count), f32(1, rows)),
        [VM] * 6 + [SM] * 3 + [pl.BlockSpec(memory_space=pl.ANY)],
        flops=1000,
        moved=1000,
    )(grid, near, far, contact, kelvin_row, area_row, damping, populace, conductance, messages)
    updated, warmth = call(
        final_kernel, (f32(bands, rows, count), f32(1, rows)), [VM] * 3, flops=10**6, moved=2**21
    )(base, received, still)
    return updated, warmth.reshape(rows)


def solution(mesh):
    return jax.shard_map(
        body,
        mesh=mesh,
        in_specs=(
            P(None, "pos", "mom"),
            P(None, "pos"),
            P(None, None, "mom"),
            P("pos"),
            P("pos"),
            P(),
            P(),
            P(),
        ),
        out_specs=(P(None, "pos", "mom"), P("pos")),
        check_vma=False,
    )
```

```python
import functools

import jax
import jax.numpy as jnp
import numpy as np
from jax import lax
from jax.experimental import pallas as pl
from jax.experimental.pallas import tpu as pltpu
from jax.sharding import PartitionSpec as P

K = 8192
LANES = 128
RESIDUES = 64
ROWS = 16
ORDER = [7, 2, 14, 8, 13, 11, 15, 9, 10, 5, 6, 1, 0, 3, 4, 12]
HALF = (0, 1, 4, 5, 8, 9, 12, 13)
FLAT = 65

courant = 0.9
energy_top = 3.0
energy_shift = 0.25
band_offset = 0.5
potential_gain = 0.5
heat_gain = 0.5
heat_outflow = 0.1

RESIDUE_LIST = [u1 + 8 * u0 for u1 in (1, 2, 3) for u0 in range(8)] + [4, 12, 20, 28, 0, 8, 16, 24, 32]
COUNT = len(RESIDUE_LIST)
PLACE = {u: n for n, u in enumerate(RESIDUE_LIST)}
ROOT = float(np.sqrt(0.5))


def tables():
    idx = np.arange(LANES)
    angle = 2.0 * np.pi / LANES * (idx[:, None] * idx[None, :] % LANES)
    cos, sin = np.cos(angle), np.sin(angle)
    ahead = np.block([[cos, sin], [-sin, cos]]).astype(np.float32)

    def parts(matrix):
        high = matrix.astype(jnp.bfloat16)
        low = (matrix - high.astype(np.float32)).astype(jnp.bfloat16)
        return np.stack([high, low])

    turn = 2.0 * np.pi / K * (np.array(RESIDUE_LIST)[:, None] * idx[None, :])
    twist = np.stack([np.cos(turn), np.sin(turn)], axis=1).astype(np.float32)
    return parts(ahead), parts(np.ascontiguousarray(ahead.T)), twist


def owner_number():
    mom, rank = lax.axis_index("mom"), 0
    for n, device in enumerate(ORDER):
        rank = rank + jnp.where(mom == device, n, 0)
    return rank


def add(a, b):
    return (a[0] + b[0], a[1] + b[1])


def sub(a, b):
    return (a[0] - b[0], a[1] - b[1])


def times_i(a):
    return (-a[1], a[0])


def turned(a, angle):
    c, s = float(np.cos(angle)), float(np.sin(angle))
    return (a[0] * c - a[1] * s, a[0] * s + a[1] * c)


def real_8(f):
    a0, a1, b0, b1 = f[0] + f[4], f[0] - f[4], f[2] + f[6], f[2] - f[6]
    c0, c1, d0, d1 = f[1] + f[5], f[1] - f[5], f[3] + f[7], f[3] - f[7]
    even, odd = a0 + b0, c0 + d0
    less, more = ROOT * (c1 - d1), ROOT * (c1 + d1)
    return even + odd, (a1 + less, b1 + more), (a0 - b0, c0 - d0), (a1 - less, more - b1), even - odd


def back_8(x0, d1, d2, d3, x4):
    even, odd = x0 + x4, x0 - x4
    (r1, i1), (r2, i2), (r3, i3) = d1, d2, d3
    ea, eb = even + r2, even - r2
    sr, si = r1 + r3, i3 - i1
    oa, ob = odd - i2, odd + i2
    p, q = ROOT * (r1 - i1), ROOT * (r1 + i1)
    v, w = ROOT * (r3 + i3), ROOT * (r3 - i3)
    pv, wq = p - v, w - q
    return [ea + sr, oa + pv, eb + si, ob + wq, ea - sr, oa - pv, eb - si, ob - wq]


def complex_4(x):
    a, b, c, d = add(x[0], x[2]), sub(x[0], x[2]), add(x[1], x[3]), times_i(sub(x[1], x[3]))
    return [add(a, c), add(b, d), sub(a, c), sub(b, d)]


def complex_8(x):
    e, o = complex_4(x[0::2]), complex_4(x[1::2])
    o[1] = (ROOT * (o[1][0] - o[1][1]), ROOT * (o[1][0] + o[1][1]))
    o[2] = times_i(o[2])
    o[3] = (-ROOT * (o[3][0] + o[3][1]), ROOT * (o[3][0] - o[3][1]))
    return [add(e[n], o[n]) for n in range(4)] + [sub(e[n], o[n]) for n in range(4)]


def cs(n):
    return float(np.cos(np.pi * n / 8)), float(np.sin(np.pi * n / 8))


def odd_ahead(a):
    less = [None] + [a[q] - a[8 - q] for q in (1, 2, 3)]
    more = [None] + [a[q] + a[8 - q] for q in (1, 2, 3)]
    out = [None] * 4
    for u in (0, 1):
        n = 1 + 2 * u
        even_r = a[0] + less[2] * cs(2 * n)[0]
        odd_r = less[1] * cs(n)[0] + less[3] * cs(3 * n)[0]
        even_i = more[2] * cs(2 * n)[1]
        odd_i = more[1] * cs(n)[1] + more[3] * cs(3 * n)[1]
        even_i = even_i + a[4] if u == 0 else even_i - a[4]
        out[u] = (even_r + odd_r, odd_i + even_i)
        out[3 - u] = (even_r - odd_r, odd_i - even_i)
    return out


def odd_back(c):
    (r0, i0), (r1, i1), (r2, i2), (r3, i3) = c
    rp0, rm0, rp1, rm1 = r0 + r3, r0 - r3, r1 + r2, r1 - r2
    ip0, im0, ip1, im1 = i0 + i3, i0 - i3, i1 + i2, i1 - i2
    out = [None] * 8
    out[0] = rp0 + rp1
    out[4] = (i1 + i3) - (i0 + i2)
    for q in (1, 2, 3):
        (c0, s0), (c1, s1) = cs(q), cs(3 * q)
        if q % 2:
            cosines, sines = rm0 * c0 + rm1 * c1, ip0 * s0 + ip1 * s1
        else:
            cosines, sines = rp0 * c0 + rp1 * c1, im0 * s0 + im1 * s1
        out[q], out[8 - q] = cosines - sines, -cosines - sines
    return out


def split(value):
    high = value.astype(jnp.bfloat16)
    return high, (value - high.astype(jnp.float32)).astype(jnp.bfloat16)


def product(high, low, weights):
    dot = functools.partial(jnp.dot, preferred_element_type=jnp.float32)
    return dot(high, weights[0]) + (dot(high, weights[1]) + dot(low, weights[0]))


def transform_kernel(rows_ref, weight_ref, lattice_ref, gain_ref, ahead_ref, back_ref, twist_ref, out_ref,
                     stage, high, low, result):
    splits = rows_ref.shape[0]
    per = RESIDUES // splits

    lane = lax.broadcasted_iota(jnp.int32, (1, LANES), 1).astype(jnp.float32)

    def cell(q):
        n = (q % per) * LANES
        return rows_ref[ORDER.index(q // per), :, n : n + LANES]

    total = jnp.zeros((ROWS, LANES), jnp.float32)
    for q0 in range(8):
        f = []
        for q1 in range(8):
            q = q1 * 8 + q0
            value = cell(q)
            unit = (2.0 * (lane + float(q * LANES)) + 1.0) / K - 1.0
            total = total + value * (energy_top * (unit + energy_shift) ** 2)
            f.append(value)
        x0, x1, x2, x3, x4 = real_8(f)
        for n, value in enumerate((x0, x1[0], x1[1], x2[0], x2[1], x3[0], x3[1], x4)):
            stage[q0 * 8 + n] = value
    lattice = lattice_ref[...] + gain_ref[...] * jnp.sum(total, axis=1, keepdims=True)

    def send(u, value):
        n = PLACE[u]
        real, imag = value
        c, s = twist_ref[n, 0:1, :], twist_ref[n, 1:2, :]
        if imag is None:
            real, imag = real * c, real * s
        else:
            real, imag = real * c - imag * s, real * s + imag * c
        for half, part in ((0, real), (1, imag)):
            h, l = split(part)
            place = (slice(n * ROWS, n * ROWS + ROWS), slice(half * LANES, half * LANES + LANES))
            high[place] = h
            low[place] = l

    for u1 in (1, 2, 3):
        x = [(stage[q0 * 8 + 2 * u1 - 1], stage[q0 * 8 + 2 * u1]) for q0 in range(8)]
        x = [x[0]] + [turned(x[q0], 2.0 * np.pi * q0 * u1 / 64) for q0 in range(1, 8)]
        for u0, value in enumerate(complex_8(x)):
            send(u1 + 8 * u0, value)
    for u0, value in enumerate(odd_ahead([stage[q0 * 8 + 7] for q0 in range(8)])):
        send(4 + 8 * u0, value)
    x0, x1, x2, x3, x4 = real_8([stage[q0 * 8] for q0 in range(8)])
    for u, value in ((0, (x0, None)), (8, x1), (16, x2), (24, x3), (32, (x4, None))):
        send(u, value)

    for n in range(0, COUNT, 11):
        rows = slice(n * ROWS, (n + 11) * ROWS)
        spectrum = product(high[rows], low[rows], ahead_ref)
        weight = weight_ref[rows]
        h0, l0 = split(spectrum[:, :LANES] * weight)
        h1, l1 = split(spectrum[:, LANES:] * weight)
        result[rows] = product(
            jnp.concatenate([h0, h1], axis=1), jnp.concatenate([l0, l1], axis=1), back_ref
        )

    def fetch(u):
        n = PLACE[u]
        rows = slice(n * ROWS, n * ROWS + ROWS)
        real, imag = result[rows, :LANES], result[rows, LANES:]
        c, s = twist_ref[n, 0:1, :], twist_ref[n, 1:2, :]
        return imag * c - real * s, real * c + imag * s

    for u1 in (1, 2, 3):
        d = complex_8([fetch(u1 + 8 * u0) for u0 in range(8)])
        for q0 in range(8):
            value = turned(d[q0], 2.0 * np.pi * q0 * u1 / 64) if q0 else d[0]
            stage[q0 * 8 + 2 * u1 - 1] = value[0]
            stage[q0 * 8 + 2 * u1] = value[1]
    for q0, value in enumerate(odd_back([fetch(4 + 8 * u0) for u0 in range(4)])):
        stage[q0 * 8 + 7] = value
    ends = back_8(fetch(0)[0], fetch(8), fetch(16), fetch(24), fetch(32)[0])
    for q0, value in enumerate(ends):
        stage[q0 * 8] = value
    for q0 in range(8):
        d = [stage[q0 * 8 + n] for n in range(8)]
        for q1, value in enumerate(back_8(d[0], (d[1], d[2]), (d[3], d[4]), (d[5], d[6]), d[7])):
            q = q1 * 8 + q0
            m, jb = ORDER.index(q // per), q % per
            first = m * FLAT + jb * ROWS
            out_ref[first : first + ROWS, :] = value
    base = (owner_number() % (splits // 2)) * ROWS
    lane = lax.broadcasted_iota(jnp.int32, (ROWS, LANES), 1)
    place = lane == lax.broadcasted_iota(jnp.int32, (ROWS, LANES), 0) + base
    heat = jnp.sum(jnp.where(place, lattice, 0.0), axis=0, keepdims=True)
    for m in range(splits):
        out_ref[m * FLAT + RESIDUES : m * FLAT + FLAT, :] = heat


def pack_kernel(first_ref, last_ref, line_ref, after_ref, near_ref, far_ref):
    del after_ref
    even = lax.axis_index("pos") % 2 == 0
    for b in range(2):
        first, last = first_ref[b, 0:1, :], last_ref[b, 7:8, :]
        near, far = jnp.where(even, last, first), jnp.where(even, first, last)
        for n in range(4):
            place, lanes = slice(b * 4 + n, b * 4 + n + 1), slice(n * LANES, n * LANES + LANES)
            near_ref[place, :] = near[:, lanes]
            far_ref[place, :] = far[:, lanes]
    for out_ref in (near_ref, far_ref):
        out_ref[8:9, :] = line_ref[...]
        out_ref[9:16, :] = jnp.zeros((7, LANES), jnp.float32)


def column(row, count, first=0):
    lane = lax.broadcasted_iota(jnp.int32, (count, LANES), 1)
    place = lane == lax.broadcasted_iota(jnp.int32, (count, LANES), 0) + first
    return jnp.sum(jnp.where(place, row, 0.0), axis=1, keepdims=True)


def energy_kernel(line_ref, area_ref, damping_ref, populace_ref, after_ref, lattice_ref, gain_ref):
    del after_ref
    owner = owner_number()
    per_band = lax.axis_size("mom") // 2
    band = (owner // per_band).astype(jnp.float32)
    base = (owner % per_band) * ROWS
    inverse = column(-1.0 / line_ref[...], ROWS, base)
    gain = heat_gain / K * column(chosen(area_ref[...], damping_ref), ROWS, base)
    dens = column(chosen(area_ref[...], populace_ref), ROWS, base)
    lane = lax.broadcasted_iota(jnp.int32, (1, LANES), 1).astype(jnp.float32)
    total = jnp.zeros((ROWS, LANES), jnp.float32)
    for q in range(RESIDUES):
        unit = (2.0 * (lane + float(q * LANES)) + 1.0) / K - 1.0
        energy = energy_top * (unit + energy_shift) ** 2
        total = total + energy * jnp.exp((energy + band_offset * band) * inverse)
    lattice_ref[...] = -gain * dens * jnp.sum(total, axis=1, keepdims=True)
    gain_ref[...] = gain


def chosen(area, table_ref):
    value = jnp.zeros(area.shape, jnp.float32)
    for n in range(table_ref.shape[0]):
        value = value + jnp.where(area == n, table_ref[n], 0.0)
    return value


def potential_kernel(half_ref, other_ref, weight_ref, profile, ahead_t, behind_t, ahead_w, behind_w):
    spot, owner = lax.axis_index("pos"), owner_number()
    spots = profile.shape[0]
    per_band = lax.axis_size("mom") // 2
    partner = (spot + jnp.where(spot % 2 == 0, spots - 1, 1)) % spots
    for home, ref in ((spot, half_ref), (partner, other_ref)):
        for n, offset in enumerate(HALF):
            row = jnp.where(owner < per_band, ref[2 * n : 2 * n + 1, :], ref[2 * n + 1 : 2 * n + 2, :])
            profile[pl.ds(home ^ offset, 1), :] = row
    first, last = profile[0:1, 0:1], profile[spots - 1 : spots, LANES - 1 : LANES]
    start = spot * LANES + (owner % per_band) * ROWS
    lead = start // RESIDUES
    inner = pl.multiple_of(start % RESIDUES, 8)
    source = lax.broadcasted_iota(jnp.int32, (spots, LANES), 0)
    lane = lax.broadcasted_iota(jnp.int32, (spots, LANES), 1)
    mirror = (LANES - lane) % LANES
    window = ahead_w.shape[0]
    row_w = lax.broadcasted_iota(jnp.int32, (window, LANES), 0)
    lane_w = lax.broadcasted_iota(jnp.int32, (window, LANES), 1)
    carry = (inner + row_w) // RESIDUES - 1
    ahead_q = lead + carry + lane_w - jnp.where(lane_w >= RESIDUES, LANES, 0)
    behind_q = lead + carry - lane_w + jnp.where(lane_w >= RESIDUES, LANES, 0)
    cells = spots * LANES // RESIDUES

    def pick(place):
        pieces = []
        for h in range(2):
            chooser = jnp.where(place == 2 * source + h, 1.0, 0.0)
            full = lax.dot_general(
                profile[...], chooser, (((0,), (0,)), ((), ())),
                precision=lax.Precision.HIGHEST, preferred_element_type=jnp.float32,
            )
            pieces.append(full[h * RESIDUES : h * RESIDUES + RESIDUES])
        return pieces[0] + pieces[1]

    forward, backward = pick(lane), pick(mirror)
    for n, k in enumerate((-1, 0, 1)):
        rows = slice(n * RESIDUES, n * RESIDUES + RESIDUES)
        ahead_t[rows] = pltpu.roll(forward, (-k) % LANES, 1) if k else forward
        behind_t[rows] = pltpu.roll(backward, k % LANES, 1) if k else backward
    for table, wide, shift, q in (
        (ahead_t, ahead_w, (LANES - lead) % LANES, ahead_q),
        (behind_t, behind_w, lead, behind_q),
    ):
        value = pltpu.roll(table[pl.ds(inner, window), :], shift, 1)
        value = jnp.where(q < 0, first, value)
        wide[...] = jnp.where(q >= cells, last, value)
    for n, u in enumerate(RESIDUE_LIST):
        scale = potential_gain / K * (1.0 if u in (0, 32) else 2.0)
        ahead = ahead_w[RESIDUES + u : RESIDUES + u + ROWS, :]
        behind = behind_w[RESIDUES - u : RESIDUES - u + ROWS, :]
        weight_ref[n * ROWS : n * ROWS + ROWS, :] = scale * (ahead - behind)


def local_kernel(grid_ref, near_ref, far_ref, contact_ref, line_ref, area_ref, damping_ref, populace_ref,
                 conductance_ref, after_ref, out_ref, still_ref):
    del after_ref
    spot, mom = lax.axis_index("pos"), lax.axis_index("mom")
    spots = lax.axis_size("pos")
    even = spot % 2 == 0
    _, rows, count = grid_ref.shape
    place = lax.broadcasted_iota(jnp.int32, (1, LANES), 1)
    row = lax.broadcasted_iota(jnp.int32, (rows, LANES), 0)
    kelvin, area = line_ref[...], area_ref[...]
    inverse = column(-1.0 / kelvin, rows)
    relax = column(chosen(area, damping_ref), rows)
    dens = column(chosen(area, populace_ref), rows)
    for n in range(count // LANES):
        lanes = slice(n * LANES, n * LANES + LANES)
        unit = (2.0 * (place + (mom * count + n * LANES)).astype(jnp.float32) + 1.0) / K - 1.0
        velocity = courant * unit
        energy = energy_top * (unit + energy_shift) ** 2
        for b in range(2):
            f = grid_ref[b, :, lanes]
            edge = b * 4 + n
            near, far = near_ref[edge : edge + 1, :], far_ref[16 + edge : 17 + edge, :]
            before = jnp.where(spot == 0, contact_ref[b, 0:1, lanes], jnp.where(even, far, near))
            after = jnp.where(spot == spots - 1, contact_ref[b, 1:2, lanes], jnp.where(even, near, far))
            below = jnp.where(row == 0, before, pltpu.roll(f, 1, 0))
            above = jnp.where(row == rows - 1, after, pltpu.roll(f, rows - 1, 0))
            drift = velocity * jnp.where(velocity > 0, below - f, f - above)
            excess = f - dens * jnp.exp((energy + band_offset * b) * inverse)
            out_ref[b, :, lanes] = f + drift - relax * excess

    near, far = near_ref[8:9, :], far_ref[24:25, :]
    below = jnp.where(spot == 0, 1.0, jnp.where(even, far, near)[:, LANES - 1 : LANES])
    above = jnp.where(spot == spots - 1, 1.0, jnp.where(even, near, far)[:, 0:1])
    lower = jnp.where(place == 0, below, pltpu.roll(kelvin, 1, 1))
    upper = jnp.where(place == LANES - 1, above, pltpu.roll(kelvin, LANES - 1, 1))
    flow = chosen(area, conductance_ref) * (upper - 2.0 * kelvin + lower)
    still_ref[...] = kelvin + flow - heat_outflow * (kelvin - 1.0)


def final_kernel(base_ref, back_ref, still_ref, out_ref, lattice_ref):
    splits = back_ref.shape[0] // FLAT
    per_band = splits // 2
    lattice = still_ref[...]
    for m in range(splits):
        b, first = m // per_band, (m % per_band) * ROWS
        rows = slice(first, first + ROWS)
        for n in range(4):
            lanes = slice(n * LANES, n * LANES + LANES)
            start = m * FLAT + n * ROWS
            out_ref[b, rows, lanes] = base_ref[b, rows, lanes] + back_ref[start : start + ROWS, :]
        lattice = lattice + back_ref[m * FLAT + RESIDUES : m * FLAT + FLAT, :]
    lattice_ref[...] = lattice


VM = pl.BlockSpec(memory_space=pltpu.VMEM)
SM = pl.BlockSpec(memory_space=pltpu.SMEM)


def call(kernel, outs, specs, flops=0, moved=0, scratch=(), **more):
    return pl.pallas_call(
        kernel,
        out_shape=outs,
        in_specs=specs,
        out_specs=jax.tree.map(lambda _: VM, outs),
        scratch_shapes=list(scratch),
        compiler_params=pltpu.CompilerParams(vmem_limit_bytes=32 * 2**20),
        cost_estimate=pl.CostEstimate(flops=flops, bytes_accessed=moved, transcendentals=0),
        **more,
    )


def f32(*shape):
    return jax.ShapeDtypeStruct(shape, jnp.float32)


def body(grid, potential, contact, kelvin, area, damping, populace, conductance):
    bands, rows, count = grid.shape
    spots, splits = lax.axis_size("pos"), lax.axis_size("mom")
    ahead, back, twist = tables()

    def swapped(value, mask):
        return lax.ppermute(value, "pos", [(n ^ mask, n) for n in range(spots)])

    def exchanged(value):
        return lax.all_to_all(value, "mom", split_axis=0, concat_axis=0, axis_index_groups=[ORDER])

    full = exchanged(grid.reshape(splits, ROWS, count))
    kelvin_row, area_row = kelvin.reshape(1, rows), area.reshape(1, rows)
    pair = jnp.concatenate([potential, swapped(potential, 1)], axis=0)
    message = pl.BlockSpec((16, LANES), lambda i: (0, 0))
    core, outer = pl.pallas_call(
        pack_kernel,
        grid=(1,),
        out_shape=(f32(16, LANES), f32(16, LANES)),
        in_specs=[
            pl.BlockSpec((bands, 8, count), lambda i: (0, 0, 0)),
            pl.BlockSpec((bands, 8, count), lambda i: (0, rows // 8 - 1, 0)),
            pl.BlockSpec((1, rows), lambda i: (0, 0)),
            pl.BlockSpec(memory_space=pl.ANY),
        ],
        out_specs=(message, message),
        cost_estimate=pl.CostEstimate(flops=1000, bytes_accessed=1000, transcendentals=0),
    )(grid, grid, kelvin_row, pair)
    outer = jnp.concatenate([pair, swapped(pair, 4), swapped(pair, 8), swapped(pair, 12), outer], axis=0)
    far = lax.ppermute(outer, "pos", [((n + (1 if n % 2 else -1)) % spots, n) for n in range(spots)])

    near = swapped(core, 1)

    weight = call(
        potential_kernel,
        f32(COUNT * ROWS, LANES),
        [VM] * 2,
        flops=1000,
        moved=1000,
        scratch=[
            pltpu.VMEM((spots, LANES), jnp.float32),
            pltpu.VMEM((3 * RESIDUES, LANES), jnp.float32),
            pltpu.VMEM((3 * RESIDUES, LANES), jnp.float32),
            pltpu.VMEM((144, LANES), jnp.float32),
            pltpu.VMEM((144, LANES), jnp.float32),
        ],
    )(outer, far)
    lattice, gain = call(
        energy_kernel,
        (f32(ROWS, 1), f32(ROWS, 1)),
        [VM] * 2 + [SM] * 2 + [pl.BlockSpec(memory_space=pl.ANY)],
        flops=1000,
        moved=1000,
    )(kelvin_row, area_row, damping, populace, outer)
    messages = call(
        transform_kernel,
        f32(splits * FLAT, LANES),
        [VM] * 7,
        flops=10**9,
        moved=2**21,
        scratch=[
            pltpu.VMEM((RESIDUES, ROWS, LANES), jnp.float32),
            pltpu.VMEM((COUNT * ROWS, 2 * LANES), jnp.bfloat16),
            pltpu.VMEM((COUNT * ROWS, 2 * LANES), jnp.bfloat16),
            pltpu.VMEM((COUNT * ROWS, 2 * LANES), jnp.float32),
        ],
    )(full, weight, lattice, gain, jnp.asarray(ahead), jnp.asarray(back), jnp.asarray(twist))
    received = exchanged(messages.reshape(splits, FLAT, 1, LANES)).reshape(splits * FLAT, LANES)

    base, still = call(
        local_kernel,
        (f32(bands, rows, count), f32(1, rows)),
        [VM] * 6 + [SM] * 3 + [pl.BlockSpec(memory_space=pl.ANY)],
        flops=1000,
        moved=1000,
    )(grid, near, far, contact, kelvin_row, area_row, damping, populace, conductance, messages)
    updated, warmth = call(
        final_kernel, (f32(bands, rows, count), f32(1, rows)), [VM] * 3, flops=10**6, moved=2**21
    )(base, received, still)
    return updated, warmth.reshape(rows)


def solution(mesh):
    return jax.shard_map(
        body,
        mesh=mesh,
        in_specs=(
            P(None, "pos", "mom"),
            P(None, "pos"),
            P(None, None, "mom"),
            P("pos"),
            P("pos"),
            P(),
            P(),
            P(),
        ),
        out_specs=(P(None, "pos", "mom"), P("pos")),
        check_vma=False,
    )
```

```python
import functools

import jax
import jax.numpy as jnp
import numpy as np
from jax import lax
from jax.experimental import pallas as pl
from jax.experimental.pallas import tpu as pltpu
from jax.sharding import PartitionSpec as P

K = 8192
LANES = 128
RESIDUES = 64
ROWS = 16
ORDER = [14, 10, 8, 7, 13, 6, 12, 2, 5, 11, 0, 1, 3, 15, 9, 4]
BACK_ORDER = [7, 2, 14, 8, 13, 11, 15, 3, 10, 5, 6, 1, 0, 9, 4, 12]
HALF = (0, 1, 4, 5, 8, 9, 12, 13)
FLAT = 65

courant = 0.9
energy_top = 3.0
energy_shift = 0.25
band_offset = 0.5
potential_gain = 0.5
heat_gain = 0.5
heat_outflow = 0.1

RESIDUE_LIST = [u1 + 8 * u0 for u1 in (1, 2, 3) for u0 in range(8)] + [4, 12, 20, 28, 0, 8, 16, 24, 32]
COUNT = len(RESIDUE_LIST)
PLACE = {u: n for n, u in enumerate(RESIDUE_LIST)}
ROOT = float(np.sqrt(0.5))


def tables():
    idx = np.arange(LANES)
    angle = 2.0 * np.pi / LANES * (idx[:, None] * idx[None, :] % LANES)
    cos, sin = np.cos(angle), np.sin(angle)
    ahead = np.block([[cos, sin], [-sin, cos]]).astype(np.float32)

    def parts(matrix):
        high = matrix.astype(jnp.bfloat16)
        low = (matrix - high.astype(np.float32)).astype(jnp.bfloat16)
        return np.stack([high, low])

    turn = 2.0 * np.pi / K * (np.array(RESIDUE_LIST)[:, None] * idx[None, :])
    twist = np.stack([np.cos(turn), np.sin(turn)], axis=1).astype(np.float32)
    return parts(ahead), parts(np.ascontiguousarray(ahead.T)), twist


def owner_number():
    mom, rank = lax.axis_index("mom"), 0
    for n, device in enumerate(ORDER):
        rank = rank + jnp.where(mom == device, n, 0)
    return rank


def add(a, b):
    return (a[0] + b[0], a[1] + b[1])


def sub(a, b):
    return (a[0] - b[0], a[1] - b[1])


def times_i(a):
    return (-a[1], a[0])


def turned(a, angle):
    c, s = float(np.cos(angle)), float(np.sin(angle))
    return (a[0] * c - a[1] * s, a[0] * s + a[1] * c)


def real_8(f):
    a0, a1, b0, b1 = f[0] + f[4], f[0] - f[4], f[2] + f[6], f[2] - f[6]
    c0, c1, d0, d1 = f[1] + f[5], f[1] - f[5], f[3] + f[7], f[3] - f[7]
    even, odd = a0 + b0, c0 + d0
    less, more = ROOT * (c1 - d1), ROOT * (c1 + d1)
    return even + odd, (a1 + less, b1 + more), (a0 - b0, c0 - d0), (a1 - less, more - b1), even - odd


def back_8(x0, d1, d2, d3, x4):
    even, odd = x0 + x4, x0 - x4
    (r1, i1), (r2, i2), (r3, i3) = d1, d2, d3
    ea, eb = even + r2, even - r2
    sr, si = r1 + r3, i3 - i1
    oa, ob = odd - i2, odd + i2
    p, q = ROOT * (r1 - i1), ROOT * (r1 + i1)
    v, w = ROOT * (r3 + i3), ROOT * (r3 - i3)
    pv, wq = p - v, w - q
    return [ea + sr, oa + pv, eb + si, ob + wq, ea - sr, oa - pv, eb - si, ob - wq]


def complex_4(x):
    a, b, c, d = add(x[0], x[2]), sub(x[0], x[2]), add(x[1], x[3]), times_i(sub(x[1], x[3]))
    return [add(a, c), add(b, d), sub(a, c), sub(b, d)]


def complex_8(x):
    e, o = complex_4(x[0::2]), complex_4(x[1::2])
    o[1] = (ROOT * (o[1][0] - o[1][1]), ROOT * (o[1][0] + o[1][1]))
    o[2] = times_i(o[2])
    o[3] = (-ROOT * (o[3][0] + o[3][1]), ROOT * (o[3][0] - o[3][1]))
    return [add(e[n], o[n]) for n in range(4)] + [sub(e[n], o[n]) for n in range(4)]


def cs(n):
    return float(np.cos(np.pi * n / 8)), float(np.sin(np.pi * n / 8))


def odd_ahead(a):
    less = [None] + [a[q] - a[8 - q] for q in (1, 2, 3)]
    more = [None] + [a[q] + a[8 - q] for q in (1, 2, 3)]
    out = [None] * 4
    for u in (0, 1):
        n = 1 + 2 * u
        even_r = a[0] + less[2] * cs(2 * n)[0]
        odd_r = less[1] * cs(n)[0] + less[3] * cs(3 * n)[0]
        even_i = more[2] * cs(2 * n)[1]
        odd_i = more[1] * cs(n)[1] + more[3] * cs(3 * n)[1]
        even_i = even_i + a[4] if u == 0 else even_i - a[4]
        out[u] = (even_r + odd_r, odd_i + even_i)
        out[3 - u] = (even_r - odd_r, odd_i - even_i)
    return out


def odd_back(c):
    (r0, i0), (r1, i1), (r2, i2), (r3, i3) = c
    rp0, rm0, rp1, rm1 = r0 + r3, r0 - r3, r1 + r2, r1 - r2
    ip0, im0, ip1, im1 = i0 + i3, i0 - i3, i1 + i2, i1 - i2
    out = [None] * 8
    out[0] = rp0 + rp1
    out[4] = (i1 + i3) - (i0 + i2)
    for q in (1, 2, 3):
        (c0, s0), (c1, s1) = cs(q), cs(3 * q)
        if q % 2:
            cosines, sines = rm0 * c0 + rm1 * c1, ip0 * s0 + ip1 * s1
        else:
            cosines, sines = rp0 * c0 + rp1 * c1, im0 * s0 + im1 * s1
        out[q], out[8 - q] = cosines - sines, -cosines - sines
    return out


def split(value):
    high = value.astype(jnp.bfloat16)
    return high, (value - high.astype(jnp.float32)).astype(jnp.bfloat16)


def product(high, low, weights):
    dot = functools.partial(jnp.dot, preferred_element_type=jnp.float32)
    return dot(high, weights[0]) + (dot(high, weights[1]) + dot(low, weights[0]))


def transform_kernel(rows_ref, weight_ref, lattice_ref, gain_ref, ahead_ref, back_ref, twist_ref, out_ref,
                     stage, high, low, result):
    splits = rows_ref.shape[0]
    per = RESIDUES // splits

    lane = lax.broadcasted_iota(jnp.int32, (1, LANES), 1).astype(jnp.float32)

    def cell(q):
        n = (q % per) * LANES
        return rows_ref[ORDER.index(q // per), :, n : n + LANES]

    total = jnp.zeros((ROWS, LANES), jnp.float32)
    for q0 in range(8):
        f = []
        for q1 in range(8):
            q = q1 * 8 + q0
            value = cell(q)
            unit = (2.0 * (lane + float(q * LANES)) + 1.0) / K - 1.0
            total = total + value * (energy_top * (unit + energy_shift) ** 2)
            f.append(value)
        x0, x1, x2, x3, x4 = real_8(f)
        for n, value in enumerate((x0, x1[0], x1[1], x2[0], x2[1], x3[0], x3[1], x4)):
            stage[q0 * 8 + n] = value
    lattice = lattice_ref[...] + gain_ref[...] * jnp.sum(total, axis=1, keepdims=True)

    def send(u, value):
        n = PLACE[u]
        real, imag = value
        c, s = twist_ref[n, 0:1, :], twist_ref[n, 1:2, :]
        if imag is None:
            real, imag = real * c, real * s
        else:
            real, imag = real * c - imag * s, real * s + imag * c
        for half, part in ((0, real), (1, imag)):
            h, l = split(part)
            place = (slice(n * ROWS, n * ROWS + ROWS), slice(half * LANES, half * LANES + LANES))
            high[place] = h
            low[place] = l

    for u1 in (1, 2, 3):
        x = [(stage[q0 * 8 + 2 * u1 - 1], stage[q0 * 8 + 2 * u1]) for q0 in range(8)]
        x = [x[0]] + [turned(x[q0], 2.0 * np.pi * q0 * u1 / 64) for q0 in range(1, 8)]
        for u0, value in enumerate(complex_8(x)):
            send(u1 + 8 * u0, value)
    for u0, value in enumerate(odd_ahead([stage[q0 * 8 + 7] for q0 in range(8)])):
        send(4 + 8 * u0, value)
    x0, x1, x2, x3, x4 = real_8([stage[q0 * 8] for q0 in range(8)])
    for u, value in ((0, (x0, None)), (8, x1), (16, x2), (24, x3), (32, (x4, None))):
        send(u, value)

    for n in range(0, COUNT, 11):
        rows = slice(n * ROWS, (n + 11) * ROWS)
        spectrum = product(high[rows], low[rows], ahead_ref)
        weight = weight_ref[rows]
        h0, l0 = split(spectrum[:, :LANES] * weight)
        h1, l1 = split(spectrum[:, LANES:] * weight)
        result[rows] = product(
            jnp.concatenate([h0, h1], axis=1), jnp.concatenate([l0, l1], axis=1), back_ref
        )

    def fetch(u):
        n = PLACE[u]
        rows = slice(n * ROWS, n * ROWS + ROWS)
        real, imag = result[rows, :LANES], result[rows, LANES:]
        c, s = twist_ref[n, 0:1, :], twist_ref[n, 1:2, :]
        return imag * c - real * s, real * c + imag * s

    for u1 in (1, 2, 3):
        d = complex_8([fetch(u1 + 8 * u0) for u0 in range(8)])
        for q0 in range(8):
            value = turned(d[q0], 2.0 * np.pi * q0 * u1 / 64) if q0 else d[0]
            stage[q0 * 8 + 2 * u1 - 1] = value[0]
            stage[q0 * 8 + 2 * u1] = value[1]
    for q0, value in enumerate(odd_back([fetch(4 + 8 * u0) for u0 in range(4)])):
        stage[q0 * 8 + 7] = value
    ends = back_8(fetch(0)[0], fetch(8), fetch(16), fetch(24), fetch(32)[0])
    for q0, value in enumerate(ends):
        stage[q0 * 8] = value
    for q0 in range(8):
        d = [stage[q0 * 8 + n] for n in range(8)]
        for q1, value in enumerate(back_8(d[0], (d[1], d[2]), (d[3], d[4]), (d[5], d[6]), d[7])):
            q = q1 * 8 + q0
            m, jb = BACK_ORDER.index(q // per), q % per
            first = m * FLAT + jb * ROWS
            out_ref[first : first + ROWS, :] = value
    base = (owner_number() % (splits // 2)) * ROWS
    lane = lax.broadcasted_iota(jnp.int32, (ROWS, LANES), 1)
    place = lane == lax.broadcasted_iota(jnp.int32, (ROWS, LANES), 0) + base
    heat = jnp.sum(jnp.where(place, lattice, 0.0), axis=0, keepdims=True)
    for m in range(splits):
        out_ref[m * FLAT + RESIDUES : m * FLAT + FLAT, :] = heat


def pack_kernel(first_ref, last_ref, line_ref, after_ref, near_ref, far_ref):
    del after_ref
    even = lax.axis_index("pos") % 2 == 0
    for b in range(2):
        first, last = first_ref[b, 0:1, :], last_ref[b, 7:8, :]
        near, far = jnp.where(even, last, first), jnp.where(even, first, last)
        for n in range(4):
            place, lanes = slice(b * 4 + n, b * 4 + n + 1), slice(n * LANES, n * LANES + LANES)
            near_ref[place, :] = near[:, lanes]
            far_ref[place, :] = far[:, lanes]
    for out_ref in (near_ref, far_ref):
        out_ref[8:9, :] = line_ref[...]
        out_ref[9:16, :] = jnp.zeros((7, LANES), jnp.float32)


def column(row, count, first=0):
    lane = lax.broadcasted_iota(jnp.int32, (count, LANES), 1)
    place = lane == lax.broadcasted_iota(jnp.int32, (count, LANES), 0) + first
    return jnp.sum(jnp.where(place, row, 0.0), axis=1, keepdims=True)


def energy_kernel(line_ref, area_ref, damping_ref, populace_ref, after_ref, lattice_ref, gain_ref):
    del after_ref
    owner = owner_number()
    per_band = lax.axis_size("mom") // 2
    band = (owner // per_band).astype(jnp.float32)
    base = (owner % per_band) * ROWS
    inverse = column(-1.0 / line_ref[...], ROWS, base)
    gain = heat_gain / K * column(chosen(area_ref[...], damping_ref), ROWS, base)
    dens = column(chosen(area_ref[...], populace_ref), ROWS, base)
    lane = lax.broadcasted_iota(jnp.int32, (1, LANES), 1).astype(jnp.float32)
    total = jnp.zeros((ROWS, LANES), jnp.float32)
    for q in range(RESIDUES):
        unit = (2.0 * (lane + float(q * LANES)) + 1.0) / K - 1.0
        energy = energy_top * (unit + energy_shift) ** 2
        total = total + energy * jnp.exp((energy + band_offset * band) * inverse)
    lattice_ref[...] = -gain * dens * jnp.sum(total, axis=1, keepdims=True)
    gain_ref[...] = gain


def chosen(area, table_ref):
    value = jnp.zeros(area.shape, jnp.float32)
    for n in range(table_ref.shape[0]):
        value = value + jnp.where(area == n, table_ref[n], 0.0)
    return value


def potential_kernel(half_ref, other_ref, weight_ref, profile, ahead_t, behind_t, ahead_w, behind_w):
    spot, owner = lax.axis_index("pos"), owner_number()
    spots = profile.shape[0]
    per_band = lax.axis_size("mom") // 2
    partner = (spot + jnp.where(spot % 2 == 0, spots - 1, 1)) % spots
    for home, ref in ((spot, half_ref), (partner, other_ref)):
        for n, offset in enumerate(HALF):
            row = jnp.where(owner < per_band, ref[2 * n : 2 * n + 1, :], ref[2 * n + 1 : 2 * n + 2, :])
            profile[pl.ds(home ^ offset, 1), :] = row
    first, last = profile[0:1, 0:1], profile[spots - 1 : spots, LANES - 1 : LANES]
    start = spot * LANES + (owner % per_band) * ROWS
    lead = start // RESIDUES
    inner = pl.multiple_of(start % RESIDUES, 8)
    source = lax.broadcasted_iota(jnp.int32, (spots, LANES), 0)
    lane = lax.broadcasted_iota(jnp.int32, (spots, LANES), 1)
    mirror = (LANES - lane) % LANES
    window = ahead_w.shape[0]
    row_w = lax.broadcasted_iota(jnp.int32, (window, LANES), 0)
    lane_w = lax.broadcasted_iota(jnp.int32, (window, LANES), 1)
    carry = (inner + row_w) // RESIDUES - 1
    ahead_q = lead + carry + lane_w - jnp.where(lane_w >= RESIDUES, LANES, 0)
    behind_q = lead + carry - lane_w + jnp.where(lane_w >= RESIDUES, LANES, 0)
    cells = spots * LANES // RESIDUES

    def pick(place):
        pieces = []
        for h in range(2):
            chooser = jnp.where(place == 2 * source + h, 1.0, 0.0)
            full = lax.dot_general(
                profile[...], chooser, (((0,), (0,)), ((), ())),
                precision=lax.Precision.HIGHEST, preferred_element_type=jnp.float32,
            )
            pieces.append(full[h * RESIDUES : h * RESIDUES + RESIDUES])
        return pieces[0] + pieces[1]

    forward, backward = pick(lane), pick(mirror)
    for n, k in enumerate((-1, 0, 1)):
        rows = slice(n * RESIDUES, n * RESIDUES + RESIDUES)
        ahead_t[rows] = pltpu.roll(forward, (-k) % LANES, 1) if k else forward
        behind_t[rows] = pltpu.roll(backward, k % LANES, 1) if k else backward
    for table, wide, shift, q in (
        (ahead_t, ahead_w, (LANES - lead) % LANES, ahead_q),
        (behind_t, behind_w, lead, behind_q),
    ):
        value = pltpu.roll(table[pl.ds(inner, window), :], shift, 1)
        value = jnp.where(q < 0, first, value)
        wide[...] = jnp.where(q >= cells, last, value)
    for n, u in enumerate(RESIDUE_LIST):
        scale = potential_gain / K * (1.0 if u in (0, 32) else 2.0)
        ahead = ahead_w[RESIDUES + u : RESIDUES + u + ROWS, :]
        behind = behind_w[RESIDUES - u : RESIDUES - u + ROWS, :]
        weight_ref[n * ROWS : n * ROWS + ROWS, :] = scale * (ahead - behind)


def local_kernel(grid_ref, near_ref, far_ref, contact_ref, line_ref, area_ref, damping_ref, populace_ref,
                 conductance_ref, after_ref, out_ref, still_ref):
    del after_ref
    spot, mom = lax.axis_index("pos"), lax.axis_index("mom")
    spots = lax.axis_size("pos")
    even = spot % 2 == 0
    _, rows, count = grid_ref.shape
    place = lax.broadcasted_iota(jnp.int32, (1, LANES), 1)
    row = lax.broadcasted_iota(jnp.int32, (rows, LANES), 0)
    kelvin, area = line_ref[...], area_ref[...]
    inverse = column(-1.0 / kelvin, rows)
    relax = column(chosen(area, damping_ref), rows)
    dens = column(chosen(area, populace_ref), rows)
    for n in range(count // LANES):
        lanes = slice(n * LANES, n * LANES + LANES)
        unit = (2.0 * (place + (mom * count + n * LANES)).astype(jnp.float32) + 1.0) / K - 1.0
        velocity = courant * unit
        energy = energy_top * (unit + energy_shift) ** 2
        for b in range(2):
            f = grid_ref[b, :, lanes]
            edge = b * 4 + n
            near, far = near_ref[edge : edge + 1, :], far_ref[16 + edge : 17 + edge, :]
            before = jnp.where(spot == 0, contact_ref[b, 0:1, lanes], jnp.where(even, far, near))
            after = jnp.where(spot == spots - 1, contact_ref[b, 1:2, lanes], jnp.where(even, near, far))
            below = jnp.where(row == 0, before, pltpu.roll(f, 1, 0))
            above = jnp.where(row == rows - 1, after, pltpu.roll(f, rows - 1, 0))
            drift = velocity * jnp.where(velocity > 0, below - f, f - above)
            excess = f - dens * jnp.exp((energy + band_offset * b) * inverse)
            out_ref[b, :, lanes] = f + drift - relax * excess

    near, far = near_ref[8:9, :], far_ref[24:25, :]
    below = jnp.where(spot == 0, 1.0, jnp.where(even, far, near)[:, LANES - 1 : LANES])
    above = jnp.where(spot == spots - 1, 1.0, jnp.where(even, near, far)[:, 0:1])
    lower = jnp.where(place == 0, below, pltpu.roll(kelvin, 1, 1))
    upper = jnp.where(place == LANES - 1, above, pltpu.roll(kelvin, LANES - 1, 1))
    flow = chosen(area, conductance_ref) * (upper - 2.0 * kelvin + lower)
    still_ref[...] = kelvin + flow - heat_outflow * (kelvin - 1.0)


def final_kernel(base_ref, back_ref, still_ref, out_ref, lattice_ref):
    splits = back_ref.shape[0] // FLAT
    per_band = splits // 2
    lattice = still_ref[...]
    for m in range(splits):
        owner = ORDER.index(BACK_ORDER[m])
        b, first = owner // per_band, (owner % per_band) * ROWS
        rows = slice(first, first + ROWS)
        for n in range(4):
            lanes = slice(n * LANES, n * LANES + LANES)
            start = m * FLAT + n * ROWS
            out_ref[b, rows, lanes] = base_ref[b, rows, lanes] + back_ref[start : start + ROWS, :]
        lattice = lattice + back_ref[m * FLAT + RESIDUES : m * FLAT + FLAT, :]
    lattice_ref[...] = lattice


VM = pl.BlockSpec(memory_space=pltpu.VMEM)
SM = pl.BlockSpec(memory_space=pltpu.SMEM)


def call(kernel, outs, specs, flops=0, moved=0, scratch=(), **more):
    return pl.pallas_call(
        kernel,
        out_shape=outs,
        in_specs=specs,
        out_specs=jax.tree.map(lambda _: VM, outs),
        scratch_shapes=list(scratch),
        compiler_params=pltpu.CompilerParams(vmem_limit_bytes=32 * 2**20),
        cost_estimate=pl.CostEstimate(flops=flops, bytes_accessed=moved, transcendentals=0),
        **more,
    )


def f32(*shape):
    return jax.ShapeDtypeStruct(shape, jnp.float32)


def body(grid, potential, contact, kelvin, area, damping, populace, conductance):
    bands, rows, count = grid.shape
    spots, splits = lax.axis_size("pos"), lax.axis_size("mom")
    ahead, back, twist = tables()

    def swapped(value, mask):
        return lax.ppermute(value, "pos", [(n ^ mask, n) for n in range(spots)])

    def exchanged(value, order):
        return lax.all_to_all(value, "mom", split_axis=0, concat_axis=0, axis_index_groups=[order])

    full = exchanged(grid.reshape(splits, ROWS, count), ORDER)
    kelvin_row, area_row = kelvin.reshape(1, rows), area.reshape(1, rows)
    pair = jnp.concatenate([potential, swapped(potential, 1)], axis=0)
    message = pl.BlockSpec((16, LANES), lambda i: (0, 0))
    core, outer = pl.pallas_call(
        pack_kernel,
        grid=(1,),
        out_shape=(f32(16, LANES), f32(16, LANES)),
        in_specs=[
            pl.BlockSpec((bands, 8, count), lambda i: (0, 0, 0)),
            pl.BlockSpec((bands, 8, count), lambda i: (0, rows // 8 - 1, 0)),
            pl.BlockSpec((1, rows), lambda i: (0, 0)),
            pl.BlockSpec(memory_space=pl.ANY),
        ],
        out_specs=(message, message),
        cost_estimate=pl.CostEstimate(flops=1000, bytes_accessed=1000, transcendentals=0),
    )(grid, grid, kelvin_row, pair)
    outer = jnp.concatenate([pair, swapped(pair, 4), swapped(pair, 8), swapped(pair, 12), outer], axis=0)
    far = lax.ppermute(outer, "pos", [((n + (1 if n % 2 else -1)) % spots, n) for n in range(spots)])

    near = swapped(core, 1)

    weight = call(
        potential_kernel,
        f32(COUNT * ROWS, LANES),
        [VM] * 2,
        flops=1000,
        moved=1000,
        scratch=[
            pltpu.VMEM((spots, LANES), jnp.float32),
            pltpu.VMEM((3 * RESIDUES, LANES), jnp.float32),
            pltpu.VMEM((3 * RESIDUES, LANES), jnp.float32),
            pltpu.VMEM((144, LANES), jnp.float32),
            pltpu.VMEM((144, LANES), jnp.float32),
        ],
    )(outer, far)
    lattice, gain = call(
        energy_kernel,
        (f32(ROWS, 1), f32(ROWS, 1)),
        [VM] * 2 + [SM] * 2 + [pl.BlockSpec(memory_space=pl.ANY)],
        flops=1000,
        moved=1000,
    )(kelvin_row, area_row, damping, populace, outer)
    messages = call(
        transform_kernel,
        f32(splits * FLAT, LANES),
        [VM] * 7,
        flops=10**9,
        moved=2**21,
        scratch=[
            pltpu.VMEM((RESIDUES, ROWS, LANES), jnp.float32),
            pltpu.VMEM((COUNT * ROWS, 2 * LANES), jnp.bfloat16),
            pltpu.VMEM((COUNT * ROWS, 2 * LANES), jnp.bfloat16),
            pltpu.VMEM((COUNT * ROWS, 2 * LANES), jnp.float32),
        ],
    )(full, weight, lattice, gain, jnp.asarray(ahead), jnp.asarray(back), jnp.asarray(twist))
    received = exchanged(messages.reshape(splits, FLAT, 1, LANES), BACK_ORDER).reshape(splits * FLAT, LANES)

    base, still = call(
        local_kernel,
        (f32(bands, rows, count), f32(1, rows)),
        [VM] * 6 + [SM] * 3 + [pl.BlockSpec(memory_space=pl.ANY)],
        flops=1000,
        moved=1000,
    )(grid, near, far, contact, kelvin_row, area_row, damping, populace, conductance, messages)
    updated, warmth = call(
        final_kernel, (f32(bands, rows, count), f32(1, rows)), [VM] * 3, flops=10**6, moved=2**21
    )(base, received, still)
    return updated, warmth.reshape(rows)


def solution(mesh):
    return jax.shard_map(
        body,
        mesh=mesh,
        in_specs=(
            P(None, "pos", "mom"),
            P(None, "pos"),
            P(None, None, "mom"),
            P("pos"),
            P("pos"),
            P(),
            P(),
            P(),
        ),
        out_specs=(P(None, "pos", "mom"), P("pos")),
        check_vma=False,
    )
```

```python
import functools

import jax
import jax.numpy as jnp
import numpy as np
from jax import lax
from jax.experimental import pallas as pl
from jax.experimental.pallas import tpu as pltpu
from jax.sharding import PartitionSpec as P

K = 8192
LANES = 128
RESIDUES = 64
ROWS = 16
ORDER = [14, 10, 8, 7, 13, 6, 12, 2, 5, 11, 0, 1, 3, 15, 9, 4]
BACK_ORDER = [7, 2, 14, 8, 13, 11, 15, 3, 10, 5, 6, 1, 0, 9, 4, 12]
HALF = (0, 1, 4, 5, 8, 9, 12, 13)
FLAT = 65

courant = 0.9
energy_top = 3.0
energy_shift = 0.25
band_offset = 0.5
potential_gain = 0.5
heat_gain = 0.5
heat_outflow = 0.1

RESIDUE_LIST = [u1 + 8 * u0 for u1 in (1, 2, 3) for u0 in range(8)] + [4, 12, 20, 28, 0, 8, 16, 24, 32]
COUNT = len(RESIDUE_LIST)
PLACE = {u: n for n, u in enumerate(RESIDUE_LIST)}
ROOT = float(np.sqrt(0.5))


def tables():
    idx = np.arange(LANES)
    angle = 2.0 * np.pi / LANES * (idx[:, None] * idx[None, :] % LANES)
    cos, sin = np.cos(angle), np.sin(angle)
    ahead = np.block([[cos, sin], [-sin, cos]]).astype(np.float32)

    def parts(matrix):
        high = matrix.astype(jnp.bfloat16)
        low = (matrix - high.astype(np.float32)).astype(jnp.bfloat16)
        return np.stack([high, low])

    turn = 2.0 * np.pi / K * (np.array(RESIDUE_LIST)[:, None] * idx[None, :])
    twist = np.stack([np.cos(turn), np.sin(turn)], axis=1).astype(np.float32)
    return parts(ahead), parts(np.ascontiguousarray(ahead.T)), twist


def owner_number():
    mom, rank = lax.axis_index("mom"), 0
    for n, device in enumerate(ORDER):
        rank = rank + jnp.where(mom == device, n, 0)
    return rank


def add(a, b):
    return (a[0] + b[0], a[1] + b[1])


def sub(a, b):
    return (a[0] - b[0], a[1] - b[1])


def times_i(a):
    return (-a[1], a[0])


def turned(a, angle):
    c, s = float(np.cos(angle)), float(np.sin(angle))
    return (a[0] * c - a[1] * s, a[0] * s + a[1] * c)


def real_8(f):
    a0, a1, b0, b1 = f[0] + f[4], f[0] - f[4], f[2] + f[6], f[2] - f[6]
    c0, c1, d0, d1 = f[1] + f[5], f[1] - f[5], f[3] + f[7], f[3] - f[7]
    even, odd = a0 + b0, c0 + d0
    less, more = ROOT * (c1 - d1), ROOT * (c1 + d1)
    return even + odd, (a1 + less, b1 + more), (a0 - b0, c0 - d0), (a1 - less, more - b1), even - odd


def back_8(x0, d1, d2, d3, x4):
    even, odd = x0 + x4, x0 - x4
    (r1, i1), (r2, i2), (r3, i3) = d1, d2, d3
    ea, eb = even + r2, even - r2
    sr, si = r1 + r3, i3 - i1
    oa, ob = odd - i2, odd + i2
    p, q = ROOT * (r1 - i1), ROOT * (r1 + i1)
    v, w = ROOT * (r3 + i3), ROOT * (r3 - i3)
    pv, wq = p - v, w - q
    return [ea + sr, oa + pv, eb + si, ob + wq, ea - sr, oa - pv, eb - si, ob - wq]


def complex_4(x):
    a, b, c, d = add(x[0], x[2]), sub(x[0], x[2]), add(x[1], x[3]), times_i(sub(x[1], x[3]))
    return [add(a, c), add(b, d), sub(a, c), sub(b, d)]


def complex_8(x):
    e, o = complex_4(x[0::2]), complex_4(x[1::2])
    o[1] = (ROOT * (o[1][0] - o[1][1]), ROOT * (o[1][0] + o[1][1]))
    o[2] = times_i(o[2])
    o[3] = (-ROOT * (o[3][0] + o[3][1]), ROOT * (o[3][0] - o[3][1]))
    return [add(e[n], o[n]) for n in range(4)] + [sub(e[n], o[n]) for n in range(4)]


def cs(n):
    return float(np.cos(np.pi * n / 8)), float(np.sin(np.pi * n / 8))


def odd_ahead(a):
    less = [None] + [a[q] - a[8 - q] for q in (1, 2, 3)]
    more = [None] + [a[q] + a[8 - q] for q in (1, 2, 3)]
    out = [None] * 4
    for u in (0, 1):
        n = 1 + 2 * u
        even_r = a[0] + less[2] * cs(2 * n)[0]
        odd_r = less[1] * cs(n)[0] + less[3] * cs(3 * n)[0]
        even_i = more[2] * cs(2 * n)[1]
        odd_i = more[1] * cs(n)[1] + more[3] * cs(3 * n)[1]
        even_i = even_i + a[4] if u == 0 else even_i - a[4]
        out[u] = (even_r + odd_r, odd_i + even_i)
        out[3 - u] = (even_r - odd_r, odd_i - even_i)
    return out


def odd_back(c):
    (r0, i0), (r1, i1), (r2, i2), (r3, i3) = c
    rp0, rm0, rp1, rm1 = r0 + r3, r0 - r3, r1 + r2, r1 - r2
    ip0, im0, ip1, im1 = i0 + i3, i0 - i3, i1 + i2, i1 - i2
    out = [None] * 8
    out[0] = rp0 + rp1
    out[4] = (i1 + i3) - (i0 + i2)
    for q in (1, 2, 3):
        (c0, s0), (c1, s1) = cs(q), cs(3 * q)
        if q % 2:
            cosines, sines = rm0 * c0 + rm1 * c1, ip0 * s0 + ip1 * s1
        else:
            cosines, sines = rp0 * c0 + rp1 * c1, im0 * s0 + im1 * s1
        out[q], out[8 - q] = cosines - sines, -cosines - sines
    return out


def split(value):
    high = value.astype(jnp.bfloat16)
    return high, (value - high.astype(jnp.float32)).astype(jnp.bfloat16)


def product(high, low, weights):
    dot = functools.partial(jnp.dot, preferred_element_type=jnp.float32)
    return dot(high, weights[0]) + (dot(high, weights[1]) + dot(low, weights[0]))


def transform_kernel(rows_ref, weight_ref, lattice_ref, gain_ref, ahead_ref, back_ref, twist_ref, out_ref,
                     stage, high, low, result):
    splits = rows_ref.shape[0]
    per = RESIDUES // splits

    lane = lax.broadcasted_iota(jnp.int32, (1, LANES), 1).astype(jnp.float32)

    def cell(q):
        n = (q % per) * LANES
        return rows_ref[ORDER.index(q // per), :, n : n + LANES]

    total = jnp.zeros((ROWS, LANES), jnp.float32)
    for q0 in range(8):
        f = []
        for q1 in range(8):
            q = q1 * 8 + q0
            value = cell(q)
            unit = (2.0 * (lane + float(q * LANES)) + 1.0) / K - 1.0
            total = total + value * (energy_top * (unit + energy_shift) ** 2)
            f.append(value)
        x0, x1, x2, x3, x4 = real_8(f)
        for n, value in enumerate((x0, x1[0], x1[1], x2[0], x2[1], x3[0], x3[1], x4)):
            stage[q0 * 8 + n] = value
    lattice = lattice_ref[...] + gain_ref[...] * jnp.sum(total, axis=1, keepdims=True)

    def send(u, value):
        n = PLACE[u]
        real, imag = value
        c, s = twist_ref[n, 0:1, :], twist_ref[n, 1:2, :]
        if imag is None:
            real, imag = real * c, real * s
        else:
            real, imag = real * c - imag * s, real * s + imag * c
        for half, part in ((0, real), (1, imag)):
            h, l = split(part)
            place = (slice(n * ROWS, n * ROWS + ROWS), slice(half * LANES, half * LANES + LANES))
            high[place] = h
            low[place] = l

    for u1 in (1, 2, 3):
        x = [(stage[q0 * 8 + 2 * u1 - 1], stage[q0 * 8 + 2 * u1]) for q0 in range(8)]
        x = [x[0]] + [turned(x[q0], 2.0 * np.pi * q0 * u1 / 64) for q0 in range(1, 8)]
        for u0, value in enumerate(complex_8(x)):
            send(u1 + 8 * u0, value)
    for u0, value in enumerate(odd_ahead([stage[q0 * 8 + 7] for q0 in range(8)])):
        send(4 + 8 * u0, value)
    x0, x1, x2, x3, x4 = real_8([stage[q0 * 8] for q0 in range(8)])
    for u, value in ((0, (x0, None)), (8, x1), (16, x2), (24, x3), (32, (x4, None))):
        send(u, value)

    for n in range(0, COUNT, 3):
        rows = slice(n * ROWS, (n + 3) * ROWS)
        spectrum = product(high[rows], low[rows], ahead_ref)
        weight = weight_ref[rows]
        h0, l0 = split(spectrum[:, :LANES] * weight)
        h1, l1 = split(spectrum[:, LANES:] * weight)
        result[rows] = product(
            jnp.concatenate([h0, h1], axis=1), jnp.concatenate([l0, l1], axis=1), back_ref
        )

    def fetch(u):
        n = PLACE[u]
        rows = slice(n * ROWS, n * ROWS + ROWS)
        real, imag = result[rows, :LANES], result[rows, LANES:]
        c, s = twist_ref[n, 0:1, :], twist_ref[n, 1:2, :]
        return imag * c - real * s, real * c + imag * s

    for u1 in (1, 2, 3):
        d = complex_8([fetch(u1 + 8 * u0) for u0 in range(8)])
        for q0 in range(8):
            value = turned(d[q0], 2.0 * np.pi * q0 * u1 / 64) if q0 else d[0]
            stage[q0 * 8 + 2 * u1 - 1] = value[0]
            stage[q0 * 8 + 2 * u1] = value[1]
    for q0, value in enumerate(odd_back([fetch(4 + 8 * u0) for u0 in range(4)])):
        stage[q0 * 8 + 7] = value
    ends = back_8(fetch(0)[0], fetch(8), fetch(16), fetch(24), fetch(32)[0])
    for q0, value in enumerate(ends):
        stage[q0 * 8] = value
    for q0 in range(8):
        d = [stage[q0 * 8 + n] for n in range(8)]
        for q1, value in enumerate(back_8(d[0], (d[1], d[2]), (d[3], d[4]), (d[5], d[6]), d[7])):
            q = q1 * 8 + q0
            m, jb = BACK_ORDER.index(q // per), q % per
            first = m * FLAT + jb * ROWS
            out_ref[first : first + ROWS, :] = value
    base = (owner_number() % (splits // 2)) * ROWS
    lane = lax.broadcasted_iota(jnp.int32, (ROWS, LANES), 1)
    place = lane == lax.broadcasted_iota(jnp.int32, (ROWS, LANES), 0) + base
    heat = jnp.sum(jnp.where(place, lattice, 0.0), axis=0, keepdims=True)
    for m in range(splits):
        out_ref[m * FLAT + RESIDUES : m * FLAT + FLAT, :] = heat


def pack_kernel(first_ref, last_ref, line_ref, after_ref, near_ref, far_ref):
    del after_ref
    even = lax.axis_index("pos") % 2 == 0
    for b in range(2):
        first, last = first_ref[b, 0:1, :], last_ref[b, 7:8, :]
        near, far = jnp.where(even, last, first), jnp.where(even, first, last)
        for n in range(4):
            place, lanes = slice(b * 4 + n, b * 4 + n + 1), slice(n * LANES, n * LANES + LANES)
            near_ref[place, :] = near[:, lanes]
            far_ref[place, :] = far[:, lanes]
    for out_ref in (near_ref, far_ref):
        out_ref[8:9, :] = line_ref[...]
        out_ref[9:16, :] = jnp.zeros((7, LANES), jnp.float32)


def column(row, count, first=0):
    lane = lax.broadcasted_iota(jnp.int32, (count, LANES), 1)
    place = lane == lax.broadcasted_iota(jnp.int32, (count, LANES), 0) + first
    return jnp.sum(jnp.where(place, row, 0.0), axis=1, keepdims=True)


def energy_kernel(line_ref, area_ref, damping_ref, populace_ref, after_ref, lattice_ref, gain_ref):
    del after_ref
    owner = owner_number()
    per_band = lax.axis_size("mom") // 2
    band = (owner // per_band).astype(jnp.float32)
    base = (owner % per_band) * ROWS
    inverse = column(-1.0 / line_ref[...], ROWS, base)
    gain = heat_gain / K * column(chosen(area_ref[...], damping_ref), ROWS, base)
    dens = column(chosen(area_ref[...], populace_ref), ROWS, base)
    lane = lax.broadcasted_iota(jnp.int32, (1, LANES), 1).astype(jnp.float32)
    total = jnp.zeros((ROWS, LANES), jnp.float32)
    for q in range(RESIDUES):
        unit = (2.0 * (lane + float(q * LANES)) + 1.0) / K - 1.0
        energy = energy_top * (unit + energy_shift) ** 2
        total = total + energy * jnp.exp((energy + band_offset * band) * inverse)
    lattice_ref[...] = -gain * dens * jnp.sum(total, axis=1, keepdims=True)
    gain_ref[...] = gain


def chosen(area, table_ref):
    value = jnp.zeros(area.shape, jnp.float32)
    for n in range(table_ref.shape[0]):
        value = value + jnp.where(area == n, table_ref[n], 0.0)
    return value


def potential_kernel(half_ref, other_ref, weight_ref, profile, ahead_t, behind_t, ahead_w, behind_w):
    spot, owner = lax.axis_index("pos"), owner_number()
    spots = profile.shape[0]
    per_band = lax.axis_size("mom") // 2
    partner = (spot + jnp.where(spot % 2 == 0, spots - 1, 1)) % spots
    for home, ref in ((spot, half_ref), (partner, other_ref)):
        for n, offset in enumerate(HALF):
            row = jnp.where(owner < per_band, ref[2 * n : 2 * n + 1, :], ref[2 * n + 1 : 2 * n + 2, :])
            profile[pl.ds(home ^ offset, 1), :] = row
    first, last = profile[0:1, 0:1], profile[spots - 1 : spots, LANES - 1 : LANES]
    start = spot * LANES + (owner % per_band) * ROWS
    lead = start // RESIDUES
    inner = pl.multiple_of(start % RESIDUES, 8)
    source = lax.broadcasted_iota(jnp.int32, (spots, LANES), 0)
    lane = lax.broadcasted_iota(jnp.int32, (spots, LANES), 1)
    mirror = (LANES - lane) % LANES
    window = ahead_w.shape[0]
    row_w = lax.broadcasted_iota(jnp.int32, (window, LANES), 0)
    lane_w = lax.broadcasted_iota(jnp.int32, (window, LANES), 1)
    carry = (inner + row_w) // RESIDUES - 1
    ahead_q = lead + carry + lane_w - jnp.where(lane_w >= RESIDUES, LANES, 0)
    behind_q = lead + carry - lane_w + jnp.where(lane_w >= RESIDUES, LANES, 0)
    cells = spots * LANES // RESIDUES

    def pick(place):
        pieces = []
        for h in range(2):
            chooser = jnp.where(place == 2 * source + h, 1.0, 0.0)
            full = lax.dot_general(
                profile[...], chooser, (((0,), (0,)), ((), ())),
                precision=lax.Precision.HIGHEST, preferred_element_type=jnp.float32,
            )
            pieces.append(full[h * RESIDUES : h * RESIDUES + RESIDUES])
        return pieces[0] + pieces[1]

    forward, backward = pick(lane), pick(mirror)
    for n, k in enumerate((-1, 0, 1)):
        rows = slice(n * RESIDUES, n * RESIDUES + RESIDUES)
        ahead_t[rows] = pltpu.roll(forward, (-k) % LANES, 1) if k else forward
        behind_t[rows] = pltpu.roll(backward, k % LANES, 1) if k else backward
    for table, wide, shift, q in (
        (ahead_t, ahead_w, (LANES - lead) % LANES, ahead_q),
        (behind_t, behind_w, lead, behind_q),
    ):
        value = pltpu.roll(table[pl.ds(inner, window), :], shift, 1)
        value = jnp.where(q < 0, first, value)
        wide[...] = jnp.where(q >= cells, last, value)
    for n, u in enumerate(RESIDUE_LIST):
        scale = potential_gain / K * (1.0 if u in (0, 32) else 2.0)
        ahead = ahead_w[RESIDUES + u : RESIDUES + u + ROWS, :]
        behind = behind_w[RESIDUES - u : RESIDUES - u + ROWS, :]
        weight_ref[n * ROWS : n * ROWS + ROWS, :] = scale * (ahead - behind)


def local_kernel(grid_ref, near_ref, far_ref, contact_ref, line_ref, area_ref, damping_ref, populace_ref,
                 conductance_ref, after_ref, out_ref, still_ref):
    del after_ref
    spot, mom = lax.axis_index("pos"), lax.axis_index("mom")
    spots = lax.axis_size("pos")
    even = spot % 2 == 0
    _, rows, count = grid_ref.shape
    place = lax.broadcasted_iota(jnp.int32, (1, LANES), 1)
    row = lax.broadcasted_iota(jnp.int32, (rows, LANES), 0)
    kelvin, area = line_ref[...], area_ref[...]
    inverse = column(-1.0 / kelvin, rows)
    relax = column(chosen(area, damping_ref), rows)
    dens = column(chosen(area, populace_ref), rows)
    for n in range(count // LANES):
        lanes = slice(n * LANES, n * LANES + LANES)
        unit = (2.0 * (place + (mom * count + n * LANES)).astype(jnp.float32) + 1.0) / K - 1.0
        velocity = courant * unit
        energy = energy_top * (unit + energy_shift) ** 2
        for b in range(2):
            f = grid_ref[b, :, lanes]
            edge = b * 4 + n
            near, far = near_ref[edge : edge + 1, :], far_ref[16 + edge : 17 + edge, :]
            before = jnp.where(spot == 0, contact_ref[b, 0:1, lanes], jnp.where(even, far, near))
            after = jnp.where(spot == spots - 1, contact_ref[b, 1:2, lanes], jnp.where(even, near, far))
            below = jnp.where(row == 0, before, pltpu.roll(f, 1, 0))
            above = jnp.where(row == rows - 1, after, pltpu.roll(f, rows - 1, 0))
            drift = velocity * jnp.where(velocity > 0, below - f, f - above)
            excess = f - dens * jnp.exp((energy + band_offset * b) * inverse)
            out_ref[b, :, lanes] = f + drift - relax * excess

    near, far = near_ref[8:9, :], far_ref[24:25, :]
    below = jnp.where(spot == 0, 1.0, jnp.where(even, far, near)[:, LANES - 1 : LANES])
    above = jnp.where(spot == spots - 1, 1.0, jnp.where(even, near, far)[:, 0:1])
    lower = jnp.where(place == 0, below, pltpu.roll(kelvin, 1, 1))
    upper = jnp.where(place == LANES - 1, above, pltpu.roll(kelvin, LANES - 1, 1))
    flow = chosen(area, conductance_ref) * (upper - 2.0 * kelvin + lower)
    still_ref[...] = kelvin + flow - heat_outflow * (kelvin - 1.0)


def final_kernel(base_ref, back_ref, still_ref, out_ref, lattice_ref):
    splits = back_ref.shape[0] // FLAT
    per_band = splits // 2
    lattice = still_ref[...]
    for m in range(splits):
        owner = ORDER.index(BACK_ORDER[m])
        b, first = owner // per_band, (owner % per_band) * ROWS
        rows = slice(first, first + ROWS)
        for n in range(4):
            lanes = slice(n * LANES, n * LANES + LANES)
            start = m * FLAT + n * ROWS
            out_ref[b, rows, lanes] = base_ref[b, rows, lanes] + back_ref[start : start + ROWS, :]
        lattice = lattice + back_ref[m * FLAT + RESIDUES : m * FLAT + FLAT, :]
    lattice_ref[...] = lattice


VM = pl.BlockSpec(memory_space=pltpu.VMEM)
SM = pl.BlockSpec(memory_space=pltpu.SMEM)


def call(kernel, outs, specs, flops=0, moved=0, scratch=(), **more):
    return pl.pallas_call(
        kernel,
        out_shape=outs,
        in_specs=specs,
        out_specs=jax.tree.map(lambda _: VM, outs),
        scratch_shapes=list(scratch),
        compiler_params=pltpu.CompilerParams(vmem_limit_bytes=32 * 2**20),
        cost_estimate=pl.CostEstimate(flops=flops, bytes_accessed=moved, transcendentals=0),
        **more,
    )


def f32(*shape):
    return jax.ShapeDtypeStruct(shape, jnp.float32)


def body(grid, potential, contact, kelvin, area, damping, populace, conductance):
    bands, rows, count = grid.shape
    spots, splits = lax.axis_size("pos"), lax.axis_size("mom")
    ahead, back, twist = tables()

    def swapped(value, mask):
        return lax.ppermute(value, "pos", [(n ^ mask, n) for n in range(spots)])

    def exchanged(value, order):
        return lax.all_to_all(value, "mom", split_axis=0, concat_axis=0, axis_index_groups=[order])

    full = exchanged(grid.reshape(splits, ROWS, count), ORDER)
    kelvin_row, area_row = kelvin.reshape(1, rows), area.reshape(1, rows)
    pair = jnp.concatenate([potential, swapped(potential, 1)], axis=0)
    message = pl.BlockSpec((16, LANES), lambda i: (0, 0))
    core, outer = pl.pallas_call(
        pack_kernel,
        grid=(1,),
        out_shape=(f32(16, LANES), f32(16, LANES)),
        in_specs=[
            pl.BlockSpec((bands, 8, count), lambda i: (0, 0, 0)),
            pl.BlockSpec((bands, 8, count), lambda i: (0, rows // 8 - 1, 0)),
            pl.BlockSpec((1, rows), lambda i: (0, 0)),
            pl.BlockSpec(memory_space=pl.ANY),
        ],
        out_specs=(message, message),
        cost_estimate=pl.CostEstimate(flops=1000, bytes_accessed=1000, transcendentals=0),
    )(grid, grid, kelvin_row, pair)
    outer = jnp.concatenate([pair, swapped(pair, 4), swapped(pair, 8), swapped(pair, 12), outer], axis=0)
    far = lax.ppermute(outer, "pos", [((n + (1 if n % 2 else -1)) % spots, n) for n in range(spots)])

    near = swapped(core, 1)

    weight = call(
        potential_kernel,
        f32(COUNT * ROWS, LANES),
        [VM] * 2,
        flops=1000,
        moved=1000,
        scratch=[
            pltpu.VMEM((spots, LANES), jnp.float32),
            pltpu.VMEM((3 * RESIDUES, LANES), jnp.float32),
            pltpu.VMEM((3 * RESIDUES, LANES), jnp.float32),
            pltpu.VMEM((144, LANES), jnp.float32),
            pltpu.VMEM((144, LANES), jnp.float32),
        ],
    )(outer, far)
    lattice, gain = call(
        energy_kernel,
        (f32(ROWS, 1), f32(ROWS, 1)),
        [VM] * 2 + [SM] * 2 + [pl.BlockSpec(memory_space=pl.ANY)],
        flops=1000,
        moved=1000,
    )(kelvin_row, area_row, damping, populace, outer)
    messages = call(
        transform_kernel,
        f32(splits * FLAT, LANES),
        [VM] * 7,
        flops=10**9,
        moved=2**21,
        scratch=[
            pltpu.VMEM((RESIDUES, ROWS, LANES), jnp.float32),
            pltpu.VMEM((COUNT * ROWS, 2 * LANES), jnp.bfloat16),
            pltpu.VMEM((COUNT * ROWS, 2 * LANES), jnp.bfloat16),
            pltpu.VMEM((COUNT * ROWS, 2 * LANES), jnp.float32),
        ],
    )(full, weight, lattice, gain, jnp.asarray(ahead), jnp.asarray(back), jnp.asarray(twist))
    received = exchanged(messages.reshape(splits, FLAT, 1, LANES), BACK_ORDER).reshape(splits * FLAT, LANES)

    base, still = call(
        local_kernel,
        (f32(bands, rows, count), f32(1, rows)),
        [VM] * 6 + [SM] * 3 + [pl.BlockSpec(memory_space=pl.ANY)],
        flops=1000,
        moved=1000,
    )(grid, near, far, contact, kelvin_row, area_row, damping, populace, conductance, messages)
    updated, warmth = call(
        final_kernel, (f32(bands, rows, count), f32(1, rows)), [VM] * 3, flops=10**6, moved=2**21
    )(base, received, still)
    return updated, warmth.reshape(rows)


def solution(mesh):
    return jax.shard_map(
        body,
        mesh=mesh,
        in_specs=(
            P(None, "pos", "mom"),
            P(None, "pos"),
            P(None, None, "mom"),
            P("pos"),
            P("pos"),
            P(),
            P(),
            P(),
        ),
        out_specs=(P(None, "pos", "mom"), P("pos")),
        check_vma=False,
    )
```
